256 devices in a mesh: req: 16 (over y, x), head: 16 (over z, core).
Axes of the slice: x: 4, y: 4, z: 8, core: 2. Of those that a mesh axis runs over, the one named last changes fastest.
Arguments:
- tokens: bfloat16 [2048, 8192], P('req', 'head'), may hold values from -6 to 6
- prior_state: float32 [32, 256, 64, 256], P('req', 'head'), may hold values from -6 to 6
- conv_inner_state: bfloat16 [32, 3, 16384], P('req', None, 'head'), may hold values from -6 to 6
- conv_group_state: bfloat16 [32, 3, 4096], P('req', None, 'head'), may hold values from -6 to 6
- gate_weight: bfloat16 [8192, 16384], P('req', 'head'), may hold values from -0.0625 to 0.0625
- inner_weight: bfloat16 [8192, 16384], P('req', 'head'), may hold values from -0.0625 to 0.0625
- group_weight: bfloat16 [8192, 4096], P('req', 'head'), may hold values from -0.0625 to 0.0625
- step_weight: bfloat16 [8192, 256], P('req', 'head'), may hold values from -0.0625 to 0.0625
- conv_inner_weight: bfloat16 [4, 16384], P(None, 'head'), may hold values from -3 to 3
- conv_inner_bias: bfloat16 [16384], P('head'), may hold values from -3 to 3
- conv_group_weight: bfloat16 [4, 4096], P(None, 'head'), may hold values from -3 to 3
- conv_group_bias: bfloat16 [4096], P('head'), may hold values from -3 to 3
- step_bias: float32 [256], P('head'), may hold values from -4 to -1
- decay_rate: float32 [256], P('head'), may hold values from 0.05 to 4
- skip_gain: float32 [256], P('head'), may hold values from 0.5 to 1.5
- norm_gain: float32 [16384], P('head'), may hold values from 0.1 to 1.9
- out_weight: bfloat16 [16384, 8192], P('head', 'req'), may hold values from -0.046875 to 0.046875
- parents: int32 [32, 64], P('req'), may hold values from -1 to 62, as said below
- accepted_path: int32 [32, 64], P('req'), may hold values from -1 to 63, as said below
- path_length: int32 [32], P('req'), may hold values from 1 to 64, as said below
- tree_size: int32 [32], P('req'), may hold values from 16 to 64, as said below
Outputs:
- mixed: bfloat16 [2048, 8192], P('req', 'head')
- next_state: float32 [32, 256, 64, 256], P('req', 'head')
The draws below stay inside these ranges and needn't reach their ends.
Inputs may be any that keep to these rules, and one draw needn't show every extreme that they name: parents[r, 0] = -1 and 0 <= parents[r, i] < i for i >= 1. accepted_path[r, 0 .. path_length - 1] runs from slot 0 to a slot below tree_size, each entry the parent of the next; later entries are -1. path_length[r] is at most tree_size[r]; some request accepts all 64 slots. `tree_size`: some tree fills all 64 slots.
All inputs are finite; a program needn't handle non-finite values.
Results may differ from the reference program's by a relative error of at most 0.017.
Values may be sent and summed in bfloat16 or wider, within the bound.
A program may use at most 192 MiB of HBM per device.

```python
import math
import jax
import jax.numpy as jnp
from jax import lax

D = 8192
HEADS = 256
HEAD_DIM = 64
STATE = 256
GROUPS = 8
CONV = 4
NODES = 64
REQUESTS = 32
TOKENS = 2048
INNER = 16384
BC = 4096


def tree_draw(key):
    first_key, second_key, third_key = jax.random.split(key, 3)
    positions = jnp.arange(NODES, dtype=jnp.int32)
    backstep = jax.random.randint(first_key, (REQUESTS, NODES), 0, 3)
    backstep = backstep.at[0].set(0)
    parents = jnp.maximum(positions[None, :] - 1 - backstep, 0)
    parents = jnp.where(positions[None, :] == 0, -1, parents).astype(jnp.int32)
    sizes = jax.random.randint(second_key, (REQUESTS,), NODES // 4, NODES + 1)
    sizes = sizes.at[0].set(NODES).astype(jnp.int32)
    leaves = jax.random.randint(third_key, (REQUESTS,), 0, sizes).astype(jnp.int32)
    leaves = leaves.at[0].set(NODES - 1).at[1].set(0).astype(jnp.int32)

    def path_of(parent_row, leaf_node):

        def climb(step_index, carry):
            marked, current = carry
            safe = jnp.maximum(current, 0)
            marked = marked.at[safe].max(jnp.where(current >= 0, 1, 0).astype(jnp.int32))
            current = jnp.where(current >= 0, parent_row[safe], -1).astype(jnp.int32)
            return (marked, current)
        marked, unused = lax.fori_loop(0, NODES, climb, (jnp.zeros(NODES, jnp.int32), leaf_node))
        order = jnp.argsort((1 - marked) * NODES + positions, stable=True).astype(jnp.int32)
        length = jnp.sum(marked).astype(jnp.int32)
        return (jnp.where(positions < length, order, -1).astype(jnp.int32), length)
    paths, lengths = jax.vmap(path_of)(parents, leaves)
    return (parents, paths, lengths, sizes)


def draw_parents(key, part):
    shared = tree_draw(key)
    return shared[0]


def draw_accepted_path(key, part):
    shared = tree_draw(key)
    return shared[1]


def draw_path_length(key, part):
    shared = tree_draw(key)
    return shared[2]


def draw_tree_size(key, part):
    shared = tree_draw(key)
    return shared[3]


def block_scale(stream_key, shape, cuts, smallest, largest):
    def one(dim, shards_of):
        steps = jax.random.uniform(jax.random.fold_in(jax.random.fold_in(stream_key, 6), dim), (shards_of,), jnp.float32, smallest / len(cuts), largest / len(cuts))
        return jnp.repeat(jnp.exp(steps), shape[dim] // shards_of).reshape((-1,) + (1,) * (len(shape) - dim - 1))

    gain = one(*cuts[0])
    for cut in cuts[1:]:
        gain = gain * one(*cut)
    return gain


def noise(own_key, extent, scale, most, cuts=(), held_as=jnp.bfloat16):
    level = block_scale(own_key, extent, cuts, -0.22, 0.18) if cuts else 1.0
    entries = jax.random.normal(own_key, extent, jnp.float32) * scale * level
    return jnp.minimum(jnp.maximum(entries, -most), most).astype(held_as)


def setup_inputs(seed: int = 0) -> dict:
    arg_keys = jax.random.split(jax.random.key(seed), 22)
    tokens = noise(arg_keys[0], (TOKENS, D), 1.0, 6.0, ((0, 16), (1, 16)))
    prior_state = noise(arg_keys[1], (REQUESTS, HEADS, HEAD_DIM, STATE), 1.0, 6.0, ((0, 16), (1, 16)), jnp.float32)
    conv_inner_state = noise(arg_keys[2], (REQUESTS, CONV - 1, INNER), 1.0, 6.0, ((0, 16), (2, 16)))
    conv_group_state = noise(arg_keys[3], (REQUESTS, CONV - 1, BC), 1.0, 6.0, ((0, 16), (2, 16)))
    gate_weight = noise(arg_keys[4], (D, INNER), D ** -0.5, 0.0625, ((0, 16), (1, 16)))
    inner_weight = noise(arg_keys[5], (D, INNER), D ** -0.5, 0.0625, ((0, 16), (1, 16)))
    group_weight = noise(arg_keys[6], (D, BC), D ** -0.5, 0.0625, ((0, 16), (1, 16)))
    step_weight = noise(arg_keys[7], (D, HEADS), D ** -0.5, 0.0625, ((0, 16), (1, 16)))
    conv_inner_weight = noise(arg_keys[8], (CONV, INNER), 0.5, 3.0, ((1, 16),))
    conv_inner_bias = noise(arg_keys[9], (INNER,), 0.5, 3.0, ((0, 16),))
    conv_group_weight = noise(arg_keys[10], (CONV, BC), 0.5, 3.0, ((1, 16),))
    conv_group_bias = noise(arg_keys[11], (BC,), 0.5, 3.0, ((0, 16),))
    step_bias = jnp.clip(-4.0 + 3.0 * jax.random.uniform(arg_keys[12], (HEADS,), jnp.float32) ** block_scale(arg_keys[12], (HEADS,), ((0, 16),), -0.2, 0.2), -4.0, -1.0)
    decay_rate = jnp.clip(jnp.exp(math.log(4.0) - 4.3820266 * jax.random.uniform(arg_keys[13], (HEADS,), jnp.float32) ** block_scale(arg_keys[13], (HEADS,), ((0, 16),), -0.2, 0.2)), 0.05, 4.0)
    skip_gain = jnp.clip(0.5 + 1.0 * jax.random.uniform(arg_keys[14], (HEADS,), jnp.float32) ** block_scale(arg_keys[14], (HEADS,), ((0, 16),), -0.2, 0.2), 0.5, 1.5)
    norm_gain = jnp.clip(1.0 + 0.18 * jax.random.normal(arg_keys[15], (INNER,), jnp.float32), 0.1, 1.9)
    out_weight = noise(arg_keys[16], (INNER, D), INNER ** -0.5, 0.046875, ((0, 16), (1, 16)))
    parents = draw_parents(jax.random.fold_in(arg_keys[21], 71), 0)
    accepted_path = draw_accepted_path(jax.random.fold_in(arg_keys[21], 71), 0)
    path_length = draw_path_length(jax.random.fold_in(arg_keys[21], 71), 0)
    tree_size = draw_tree_size(jax.random.fold_in(arg_keys[21], 71), 0)
    return {"tokens": tokens, "prior_state": prior_state, "conv_inner_state": conv_inner_state, "conv_group_state": conv_group_state, "gate_weight": gate_weight, "inner_weight": inner_weight, "group_weight": group_weight, "step_weight": step_weight, "conv_inner_weight": conv_inner_weight, "conv_inner_bias": conv_inner_bias, "conv_group_weight": conv_group_weight, "conv_group_bias": conv_group_bias, "step_bias": step_bias, "decay_rate": decay_rate, "skip_gain": skip_gain, "norm_gain": norm_gain, "out_weight": out_weight, "parents": parents, "accepted_path": accepted_path, "path_length": path_length, "tree_size": tree_size}


HIGHEST_PRECISION = lax.Precision.HIGHEST

def tree_maps(parents):
    node_count = parents.shape[1]
    positions = jnp.arange(node_count, dtype=jnp.int32)
    parent_map = (parents[:, :, None] == positions[None, None, :]).astype(jnp.float32)
    reach = jnp.eye(node_count, dtype=jnp.float32)[None] + parent_map
    for sweep in range(6):
        reach = jnp.minimum(jnp.einsum('rij,rjk->rik', reach, reach, precision=HIGHEST_PRECISION), 1.0)
    node_depth = lax.optimization_barrier(jnp.sum(reach, axis=-1)) - 1.0
    return (parent_map, reach, node_depth)

def tree_conv(values, prior_inputs, parent_map, node_depth, taps, offset):
    values = values.astype(jnp.float32)
    prior_inputs = prior_inputs.astype(jnp.float32)
    taps = taps.astype(jnp.float32)
    summed = offset.astype(jnp.float32) + taps[CONV - 1] * values
    ancestor_step = jnp.broadcast_to(jnp.eye(parent_map.shape[1], dtype=jnp.float32), parent_map.shape)
    slot_index = jnp.arange(CONV - 1, dtype=jnp.float32)
    for lag_index in range(1, CONV):
        ancestor_step = jnp.einsum('rij,rjk->rik', ancestor_step, parent_map, precision=HIGHEST_PRECISION)
        earlier = (lag_index > node_depth)[..., None] & (slot_index[None, None, :] == CONV - 1 - lag_index + node_depth[..., None])
        lagged = jnp.einsum('rij,rjc->ric', ancestor_step, values, precision=HIGHEST_PRECISION)
        lagged = lagged + jnp.einsum('ris,rsc->ric', earlier.astype(jnp.float32), prior_inputs, precision=HIGHEST_PRECISION)
        summed = summed + taps[CONV - 1 - lag_index] * lagged
    return jax.nn.silu(summed)

def reference(tokens, prior_state, conv_inner_state, conv_group_state, gate_weight, inner_weight, group_weight, step_weight, conv_inner_weight, conv_inner_bias, conv_group_weight, conv_group_bias, step_bias, decay_rate, skip_gain, norm_gain, out_weight, parents, accepted_path, path_length, tree_size):

    def project(weights):
        return jnp.dot(tokens, weights, preferred_element_type=jnp.float32).astype(jnp.bfloat16)
    gate_raw = project(gate_weight).reshape(REQUESTS, NODES, INNER)
    inner_raw = project(inner_weight).reshape(REQUESTS, NODES, INNER)
    group_raw = project(group_weight).reshape(REQUESTS, NODES, BC)
    step_raw = project(step_weight).reshape(REQUESTS, NODES, HEADS)
    parent_map, reach, node_depth = tree_maps(parents)
    channels = tree_conv(inner_raw, conv_inner_state, parent_map, node_depth, conv_inner_weight, conv_inner_bias)
    group_values = tree_conv(group_raw, conv_group_state, parent_map, node_depth, conv_group_weight, conv_group_bias)
    group_values = group_values.reshape(REQUESTS, NODES, GROUPS, 2, STATE)
    b_heads = jnp.repeat(group_values[:, :, :, 0], HEADS // GROUPS, axis=2)
    c_heads = jnp.repeat(group_values[:, :, :, 1], HEADS // GROUPS, axis=2)
    heads_x = channels.reshape(REQUESTS, NODES, HEADS, HEAD_DIM)
    step_size = jax.nn.softplus(step_raw.astype(jnp.float32) + step_bias)
    log_decay = -decay_rate * step_size
    cumulative = jnp.einsum('rij,rjh->rih', reach, log_decay, precision=HIGHEST_PRECISION)
    gap = cumulative[:, :, None, :] - cumulative[:, None, :, :]
    decays = jnp.where(reach[..., None] > 0, jnp.exp(jnp.minimum(gap, 0.0)), 0.0)
    intersection = jnp.einsum('rihn,rjhn->rijh', c_heads, b_heads, precision=HIGHEST_PRECISION)
    mixing = decays * intersection * step_size[:, None, :, :]
    output = jnp.einsum('rijh,rjhp->rihp', mixing, heads_x, precision=HIGHEST_PRECISION)
    output = output + jnp.exp(cumulative)[..., None] * jnp.einsum('rihn,rhpn->rihp', c_heads, prior_state, precision=HIGHEST_PRECISION)
    output = output + skip_gain[None, None, :, None] * heads_x
    valid = jnp.arange(NODES, dtype=jnp.int32)[None, :] < tree_size[:, None]
    output = jnp.where(valid[:, :, None, None], output, 0.0).reshape(REQUESTS, NODES, INNER)
    gated = output * jax.nn.silu(gate_raw.astype(jnp.float32))
    grouped = gated.reshape(REQUESTS, NODES, GROUPS, INNER // GROUPS)
    mean_square = lax.optimization_barrier(jnp.mean(grouped * grouped, axis=-1, keepdims=True))
    normed = (grouped * lax.rsqrt(mean_square + 1e-05)).reshape(REQUESTS, NODES, INNER) * norm_gain
    normed = normed.astype(jnp.bfloat16).reshape(TOKENS, INNER)
    mixed = jnp.dot(normed, out_weight, preferred_element_type=jnp.float32).astype(jnp.bfloat16)

    def advance(step_index, state_now):
        chosen = jnp.maximum(accepted_path[:, step_index], 0).astype(jnp.int32)
        live = step_index < path_length
        x_node = jnp.take_along_axis(heads_x, chosen[:, None, None, None], axis=1)[:, 0]
        b_node = jnp.take_along_axis(b_heads, chosen[:, None, None, None], axis=1)[:, 0]
        decay_node = jnp.take_along_axis(log_decay, chosen[:, None, None], axis=1)[:, 0]
        size_node = jnp.take_along_axis(step_size, chosen[:, None, None], axis=1)[:, 0]
        moved = jnp.exp(decay_node)[:, :, None, None] * state_now + size_node[:, :, None, None] * x_node[:, :, :, None] * b_node[:, :, None, :]
        return jnp.where(live[:, None, None, None], moved, state_now)
    next_state = lax.fori_loop(0, NODES, advance, prior_state)
    return (mixed, next_state)
```

```python
import functools

import jax
import jax.numpy as jnp
from jax import lax
from jax.experimental import pallas as pl
from jax.experimental.pallas import tpu as pltpu
from jax.sharding import PartitionSpec as P

HEAD_DIM = 64
STATE = 256
GROUPS = 8
CONV = 4
INNER = 16384
MESH = pl.DeviceIdType.MESH
F32 = jnp.float32
BF16 = jnp.bfloat16
HIGHEST_PRECISION = lax.Precision.HIGHEST
UNITS = (
    ("group", 0, 128, 128),
    ("inner", 0, 512, 256),
    ("inner", 256, 768, 256),
    ("gate", 0, 512, 256),
    ("gate", 256, 768, 256),
)


class Place:
    def __init__(self):
        self.r = lax.axis_index("req")
        self.h = lax.axis_index("head")
        self.y, self.x = self.r // 4, self.r % 4
        self.z, self.c = self.h // 2, self.h % 2

    def at(self, dy=0, dx=0, dz=0, dc=0):
        y, x = (self.y + dy) % 4, (self.x + dx) % 4
        z, c = (self.z + dz) % 8, (self.c + dc) % 2
        return (y * 4 + x, z * 2 + c)


def remote(src, dst, send, recv, device):
    return pltpu.make_async_remote_copy(
        src_ref=src, dst_ref=dst, send_sem=send, recv_sem=recv,
        device_id=device, device_id_type=MESH,
    )


def meet(devices, maybe=()):
    barrier = pltpu.get_barrier_semaphore()
    for device in devices:
        pl.semaphore_signal(barrier, inc=1, device_id=device, device_id_type=MESH)
    for device, here in maybe:
        @pl.when(here)
        def _():
            pl.semaphore_signal(barrier, inc=1, device_id=device, device_id_type=MESH)
    pl.semaphore_wait(barrier, len(devices) + sum(jnp.where(here, 1, 0) for _, here in maybe))


def dot(a, b):
    return jnp.dot(a, b, preferred_element_type=F32)


class Unit:
    def __init__(self, place, first, weight, column, width, tokens, out, bufs, send, recv):
        self.p, self.first = place, first
        self.a, self.b = (place.x, place.y) if first == "x" else (place.y, place.x)
        self.weight, self.column, self.width = weight, column, width
        self.tokens, self.out = tokens, out
        (self.s1, self.rf, self.s2p, self.s2m, self.rgp, self.rgm, self.q,
         self.s3, self.rh, self.s4p, self.s4m, self.rip, self.rim) = bufs
        self.send, self.recv = send, recv
        self.copies = {}

    def along(self, which, step):
        name = self.first if which == "a" else ("y" if self.first == "x" else "x")
        return self.p.at(dy=step) if name == "y" else self.p.at(dx=step)

    def part(self, dest_a, b):
        slot = 4 * b + dest_a if self.first == "x" else 4 * dest_a + b
        return dot(
            self.tokens[slot], self.weight[:, self.column : self.column + self.width]
        )

    def put(self, k, src, dst, which, step):
        copy = remote(src, dst, self.send.at[k], self.recv.at[k], self.along(which, step))
        copy.start()
        self.copies[k] = copy

    def stage1(self):
        far = (self.a + 2) % 4

        @pl.loop(0, 4)
        def _(b):
            self.s1[b] = self.part(far, b).astype(BF16)

        self.put(0, self.s1.at[0:2], self.rf.at[0:2], "a", 1)
        self.put(1, self.s1.at[2:4], self.rf.at[2:4], "a", -1)

    def stage2(self):
        self.copies[0].wait_recv()
        self.copies[1].wait_recv()
        up, down = (self.a + 1) % 4, (self.a + 3) % 4

        @pl.loop(0, 2)
        def _(b):
            self.s2p[b] = (self.part(up, b) + self.rf[b].astype(F32)).astype(BF16)
            self.s2p[b + 2] = self.part(up, b + 2).astype(BF16)
            self.s2m[b] = self.part(down, b).astype(BF16)
            self.s2m[b + 2] = (self.part(down, b + 2) + self.rf[b + 2].astype(F32)).astype(BF16)

        self.put(2, self.s2p, self.rgp, "a", 1)
        self.put(3, self.s2m, self.rgm, "a", -1)

    def stage3(self):
        self.copies[2].wait_recv()
        self.copies[3].wait_recv()

        @pl.loop(0, 4)
        def _(b):
            self.q[b] = self.part(self.a, b) + self.rgp[b].astype(F32) + self.rgm[b].astype(F32)

        self.s3[...] = self.q[(self.b + 2) % 4].astype(BF16)
        self.put(4, self.s3.at[0:64], self.rh.at[0:64], "b", 1)
        self.put(5, self.s3.at[64:128], self.rh.at[64:128], "b", -1)

    def stage4(self):
        self.copies[4].wait_recv()
        self.copies[5].wait_recv()
        up, down = (self.b + 1) % 4, (self.b + 3) % 4
        self.s4p[0:64] = (self.q[up, 0:64] + self.rh[0:64].astype(F32)).astype(BF16)
        self.s4p[64:128] = self.q[up, 64:128].astype(BF16)
        self.s4m[0:64] = self.q[down, 0:64].astype(BF16)
        self.s4m[64:128] = (self.q[down, 64:128] + self.rh[64:128].astype(F32)).astype(BF16)
        self.put(6, self.s4p, self.rip, "b", 1)
        self.put(7, self.s4m, self.rim, "b", -1)

    def stage5(self):
        self.copies[6].wait_recv()
        self.copies[7].wait_recv()
        total = self.q[self.b] + self.rip[...].astype(F32) + self.rim[...].astype(F32)
        self.out[:, self.column : self.column + self.width] = total.astype(BF16)

    def finish(self):
        for copy in self.copies.values():
            copy.wait_send()


def unit_scratch(width):
    def block(n, dtype=BF16):
        return pltpu.VMEM((n, 128, width), dtype)

    flat = pltpu.VMEM((128, width), BF16)
    return [block(4)] * 6 + [block(4, F32)] + [flat] * 6


def input_kernel(*refs):
    (tok, wgate, winner, wgroup, wstep, wout,
     gate, inner, group, step, wx, wy,
     tg, st, sr,
     tsem_s, tsem_r, zs, zr, cs, cr, ss, sr_sem, os, orr, gs, gr, us, ur, local) = refs[:30]
    bufs = refs[30:]
    p = Place()
    r, h, z, c = p.r, p.h, p.z, p.c
    other = (h // 4) * 4 + h % 4
    moved = r != h
    req_peers = [((r + j) % 16, h) for j in range(1, 16)]
    meet(
        req_peers + [p.at(dz=1), p.at(dz=-1), p.at(dc=1)],
        [((other, r), moved)],
    )
    turn = remote(tok, tg.at[r], tsem_s, tsem_r, (other, r))

    @pl.when(moved)
    def _():
        turn.start()

    @pl.when(jnp.logical_not(moved))
    def _():
        pltpu.make_async_copy(tok, tg.at[r], local).start()

    outs = []
    for ax, full, lo in (("x", wx, 0), ("y", wy, 256)):
        me = p.x if ax == "x" else p.y
        half = wout.at[:, lo : lo + 256]
        for i, d in enumerate((1, -1)):
            peer = p.at(dx=d) if ax == "x" else p.at(dy=d)
            k = len(outs)
            copy = remote(half, full.at[me], os.at[k], orr.at[k], peer)
            copy.start()
            outs.append(copy)
        keep = pltpu.make_async_copy(half, full.at[me], os.at[len(outs) + 6])
        keep.start()
        outs.append(keep)

    @pl.when(moved)
    def _():
        turn.wait()

    @pl.when(jnp.logical_not(moved))
    def _():
        pltpu.make_async_copy(tok, tg.at[r], local).wait()

    def block(dz):
        return 2 * ((z + dz) % 8) + c

    cores = []

    def to_core(dz):
        k = len(cores)
        copy = remote(tg.at[block(dz)], tg.at[block(dz)], cs.at[k], cr.at[k], p.at(dc=1))
        copy.start()
        cores.append(copy)

    ring = []

    def hop(dz, d, lo, n):
        k = len(ring)
        ref = tg.at[block(dz), lo : lo + n]
        copy = remote(ref, ref, zs.at[k], zr.at[k], p.at(dz=d))
        copy.start()
        ring.append(copy)
        return copy

    plus, minus = hop(0, 1, 0, 128), hop(0, -1, 0, 128)
    to_core(0)
    for s in range(1, 4):
        rows = 128 if s < 3 else 64
        plus.wait_recv()
        plus = hop(-s, 1, 0, rows)
        minus.wait_recv()
        minus = hop(s, -1, 128 - rows, rows)
        to_core(-s)
        to_core(s)
    plus.wait_recv()
    minus.wait_recv()
    to_core(4)
    for k, (ax, full, d, lo) in enumerate(
        (("x", wx, 1, 0), ("x", wx, -1, 512), ("y", wy, 1, 0), ("y", wy, -1, 512))
    ):
        first = outs[(0, 1, 3, 4)[k]]
        first.wait_recv()
        me = p.x if ax == "x" else p.y
        peer = p.at(dx=d) if ax == "x" else p.at(dy=d)
        ref = full.at[(me - d) % 4, lo : lo + 512]
        copy = remote(ref, ref, gs.at[k], gr.at[k], peer)
        copy.start()
        outs.append(copy)
    for copy in cores:
        copy.wait_recv()

    @pl.loop(0, 16)
    def _(k):
        st[k] = lax.dot_general(
            wstep[...], tg[k], (((1,), (1,)), ((), ())), preferred_element_type=F32
        )

    @pl.loop(1, 16)
    def _(j):
        to = (r + j) % 16
        remote(st.at[to], sr.at[j], ss, sr_sem, (to, h)).start()

    sources = {"group": wgroup, "inner": winner, "gate": wgate}
    results = {"group": group, "inner": inner, "gate": gate}
    units = []
    for i, (name, xcol, ycol, width) in enumerate(UNITS):
        pair = []
        for j, (first, col) in enumerate((("x", xcol), ("y", ycol))):
            n = 2 * i + j
            out = group.at[p.c] if name == "group" else results[name]
            pair.append(Unit(p, first, sources[name], col, width, tg, out,
                             bufs[13 * n : 13 * n + 13], us.at[n], ur.at[n]))
        units.append(pair)
    count = len(units)
    swap = remote(group.at[p.c], group.at[p.c], tsem_s, tsem_r, p.at(dc=1))
    for t in range(-1, count + 3):
        for stage, lag in ((1, -1), (2, 0), (3, 1), (4, 2), (5, 3)):
            if 0 <= t - lag < count:
                for unit in units[t - lag]:
                    getattr(unit, "stage%d" % stage)()
                if stage == 5 and t - lag == 0:
                    swap.start()
    for pair in units:
        for unit in pair:
            unit.finish()
    swap.wait()
    tail = sr.at[1:16]
    pltpu.make_async_copy(tail, tail, sr_sem).wait()
    sums = st[r]
    for j in range(1, 16):
        sums = sums + sr[j]
    step[...] = sums
    pltpu.make_async_copy(tail, tail, ss).wait()
    for k, copy in enumerate(outs):
        if k in (2, 5):
            copy.wait()
        else:
            copy.wait_send()
            if k > 5:
                copy.wait_recv()
    for copy in cores + ring:
        copy.wait_send()


def project(tokens, wgate, winner, wgroup, wstep_t, wout):
    vmem = pl.BlockSpec(memory_space=pltpu.VMEM)
    hbm = pl.BlockSpec(memory_space=pl.ANY)
    dma = pltpu.SemaphoreType.DMA
    scratch = [
        pltpu.VMEM((16, 128, 512), BF16),
        pltpu.VMEM((16, 16, 128), F32),
        pltpu.VMEM((16, 16, 128), F32),
        dma, dma, dma((8,)), dma((8,)), dma((8,)), dma((8,)), dma, dma,
        dma((12,)), dma((6,)), dma((4,)), dma((4,)),
        dma((2 * len(UNITS), 8)), dma((2 * len(UNITS), 8)), dma,
    ]
    for _, _, _, width in UNITS:
        scratch += unit_scratch(width) * 2
    shape = jax.ShapeDtypeStruct
    return pl.pallas_call(
        input_kernel,
        name="input_projections",
        out_shape=(
            shape((128, 1024), BF16), shape((128, 1024), BF16), shape((2, 128, 256), BF16),
            shape((16, 128), F32), shape((4, 1024, 256), BF16), shape((4, 1024, 256), BF16),
        ),
        in_specs=[vmem] * 5 + [hbm],
        out_specs=(vmem,) * 4 + (hbm,) * 2,
        scratch_shapes=scratch,
        compiler_params=pltpu.CompilerParams(
            collective_id=0, has_side_effects=True, vmem_limit_bytes=56 * 2**20
        ),
    )(tokens, wgate, winner, wgroup, wstep_t, wout)


def output_kernel(norm, wx, wy, out,
                  nx, ny, own, sent, got, zsend_p, zsend_m, zgot_p, zgot_m, fin, land,
                  ns, nr, cs, cr, zs, zr, fs, fr, local):
    p = Place()
    r, h, y, x, z, c = p.r, p.h, p.y, p.x, p.z, p.c
    hy, hx = h // 4, h % 4
    goal = ((hy * 4 + x, y * 4 + hx), (y * 4 + hx, hy * 4 + x))
    away = (hy != y, hx != x)
    meet(
        [p.at(dy=d) for d in (1, 2, 3)] + [p.at(dx=d) for d in (1, 2, 3)]
        + [p.at(dz=1), p.at(dz=-1), p.at(dc=1)],
        [(goal[0], away[0]), (goal[1], away[1])],
    )
    copies = []
    for d in (1, 3, 2):
        for full, peer in ((ny.at[y], p.at(dy=d)), (nx.at[x], p.at(dx=d))):
            k = len(copies)
            copy = remote(norm, full, ns.at[k], nr.at[k], peer)
            copy.start()
            copies.append(copy)
    nx[x] = norm[...]
    ny[y] = norm[...]

    def shard(zz, cc):
        s = 2 * zz + cc
        i, j = s // 4, s % 4
        return dot(ny[i], wx[j]), dot(nx[j], wy[i])

    for copy in copies:
        copy.wait_recv()

    @pl.loop(0, 8)
    def _(zz):
        left, right = shard(zz, 1 - c)
        sent[zz, 0] = left.astype(BF16)
        sent[zz, 1] = right.astype(BF16)

    swap = remote(sent, got, cs, cr, p.at(dc=1))
    swap.start()

    @pl.loop(0, 8)
    def _(zz):
        left, right = shard(zz, c)
        own[zz, 0] = left
        own[zz, 1] = right

    swap.wait_recv()

    def mine(dz, half):
        zz = (z + dz) % 8
        return own[zz, half] + got[zz, half].astype(F32)

    ring = []

    def hop(src, dst, d):
        k = len(ring)
        copy = remote(src, dst, zs.at[k], zr.at[k], p.at(dz=d))
        copy.start()
        ring.append(copy)
        return copy

    zsend_p[0, 0] = mine(4, 0).astype(BF16)
    plus = hop(zsend_p.at[0, 0], zgot_p.at[0, 0], 1)
    zsend_m[0, 1] = mine(4, 1).astype(BF16)
    minus = hop(zsend_m.at[0, 1], zgot_m.at[0, 1], -1)
    for s in (1, 2, 3):
        plus.wait_recv()
        zsend_p[s, 0] = (mine(4 - s, 0) + zgot_p[s - 1, 0].astype(F32)).astype(BF16)
        if s == 1:
            zsend_p[s, 1] = mine(4 - s, 1).astype(BF16)
        else:
            zsend_p[s, 1] = (mine(4 - s, 1) + zgot_p[s - 1, 1].astype(F32)).astype(BF16)
        plus = hop(zsend_p.at[s], zgot_p.at[s], 1)
        minus.wait_recv()
        if s == 1:
            zsend_m[s, 0] = mine(s - 4, 0).astype(BF16)
        else:
            zsend_m[s, 0] = (mine(s - 4, 0) + zgot_m[s - 1, 0].astype(F32)).astype(BF16)
        zsend_m[s, 1] = (mine(s - 4, 1) + zgot_m[s - 1, 1].astype(F32)).astype(BF16)
        minus = hop(zsend_m.at[s], zgot_m.at[s], -1)
    plus.wait_recv()
    minus.wait_recv()
    for half in (0, 1):
        fin[half] = (
            mine(0, half) + zgot_p[3, half].astype(F32) + zgot_m[3, half].astype(F32)
        ).astype(BF16)
        move = remote(fin.at[half], land.at[half], fs.at[half], fr.at[half], goal[half])

        @pl.when(away[half])
        def _():
            move.start()

        @pl.when(jnp.logical_not(away[half]))
        def _():
            land[half] = fin[half]

    for half in (0, 1):
        move = remote(fin.at[half], land.at[half], fs.at[half], fr.at[half], goal[half])

        @pl.when(away[half])
        def _():
            move.wait()

        out[:, 256 * half : 256 * half + 256] = land[half]
    for copy in copies + ring + [swap]:
        copy.wait_send()


def finish(normed, wx, wy):
    vmem = pl.BlockSpec(memory_space=pltpu.VMEM)
    dma = pltpu.SemaphoreType.DMA
    return pl.pallas_call(
        output_kernel,
        name="output_projection",
        out_shape=jax.ShapeDtypeStruct((128, 512), BF16),
        in_specs=[vmem] * 3,
        out_specs=vmem,
        scratch_shapes=[
            pltpu.VMEM((4, 128, 1024), BF16), pltpu.VMEM((4, 128, 1024), BF16),
            pltpu.VMEM((8, 2, 128, 256), F32),
            pltpu.VMEM((8, 2, 128, 256), BF16), pltpu.VMEM((8, 2, 128, 256), BF16),
            pltpu.VMEM((4, 2, 128, 256), BF16), pltpu.VMEM((4, 2, 128, 256), BF16),
            pltpu.VMEM((4, 2, 128, 256), BF16), pltpu.VMEM((4, 2, 128, 256), BF16),
            pltpu.VMEM((2, 128, 256), BF16), pltpu.VMEM((2, 128, 256), BF16),
            dma((6,)), dma((6,)), dma, dma, dma((8,)), dma((8,)), dma((2,)), dma((2,)), dma,
        ],
        compiler_params=pltpu.CompilerParams(
            collective_id=1, has_side_effects=True, vmem_limit_bytes=48 * 2**20
        ),
    )(normed, wx, wy)


def from_partner(block, axis, stride):
    count = lax.axis_size(axis)
    route = []
    for low in range(count):
        high = low | 1 << stride
        if high != low and high < count:
            route += [(low, high), (high, low)]
    return lax.ppermute(block, axis, route)


def tree_maps(parents):
    node_count = parents.shape[1]
    positions = jnp.arange(node_count, dtype=jnp.int32)
    parent_map = (parents[:, :, None] == positions[None, None, :]).astype(jnp.float32)
    reach = jnp.eye(node_count, dtype=jnp.float32)[None] + parent_map
    for sweep in range(6):
        reach = jnp.minimum(
            jnp.einsum("rij,rjk->rik", reach, reach, precision=HIGHEST_PRECISION), 1.0
        )
    node_depth = jnp.sum(reach, axis=-1) - 1.0
    return (parent_map, reach, node_depth)


def tree_conv(values, prior_inputs, parent_map, node_depth, taps, offset):
    values = values.astype(jnp.float32)
    prior_inputs = prior_inputs.astype(jnp.float32)
    taps = taps.astype(jnp.float32)
    summed = offset.astype(jnp.float32) + taps[CONV - 1] * values
    ancestor_step = jnp.broadcast_to(
        jnp.eye(parent_map.shape[1], dtype=jnp.float32), parent_map.shape
    )
    slot_index = jnp.arange(CONV - 1, dtype=jnp.float32)
    for lag_index in range(1, CONV):
        ancestor_step = jnp.einsum(
            "rij,rjk->rik", ancestor_step, parent_map, precision=HIGHEST_PRECISION
        )
        earlier = (lag_index > node_depth)[..., None] & (
            slot_index[None, None, :] == CONV - 1 - lag_index + node_depth[..., None]
        )
        lagged = jnp.einsum("rij,rjc->ric", ancestor_step, values, precision=HIGHEST_PRECISION)
        lagged = lagged + jnp.einsum(
            "ris,rsc->ric", earlier.astype(jnp.float32), prior_inputs, precision=HIGHEST_PRECISION
        )
        summed = summed + taps[CONV - 1 - lag_index] * lagged
    return jax.nn.silu(summed)


def join_halves(mine, partner, upper_half):
    return jnp.where(
        upper_half == 1,
        jnp.concatenate((partner, mine), axis=-1),
        jnp.concatenate((mine, partner), axis=-1),
    )


def on_device(
    tokens, prior_state, conv_inner_state, conv_group_state, gate_weight, inner_weight,
    group_weight, step_weight, conv_inner_weight, conv_inner_bias, conv_group_weight,
    conv_group_bias, step_bias, decay_rate, skip_gain, norm_gain, out_weight, parents,
    accepted_path, path_length, tree_size,
):
    request_count, node_count = parents.shape
    token_rows = tokens.shape[0]
    position = lax.axis_index("head")
    parent_map, reach, node_depth = tree_maps(parents)
    group_parts = (conv_group_weight, conv_group_bias, conv_group_state)
    partner = jax.tree.map(lambda part: from_partner(part, "head", 0), group_parts)
    upper_half = position & 1
    group_taps, group_bias, group_state = (
        join_halves(mine, other_part, upper_half)
        for mine, other_part in zip(group_parts, partner)
    )
    gate_raw, inner_raw, group_raw, step_raw, wx, wy = project(
        tokens, gate_weight, inner_weight, group_weight, step_weight.T, out_weight
    )
    shaped = (request_count, node_count, -1)
    gate_raw, inner_raw = gate_raw.reshape(shaped), inner_raw.reshape(shaped)
    group_raw = jnp.concatenate((group_raw[0], group_raw[1]), axis=-1).reshape(shaped)
    step_raw = step_raw.astype(BF16).T.reshape(shaped)
    group_values = tree_conv(
        group_raw, group_state, parent_map, node_depth, group_taps, group_bias
    )
    channels = tree_conv(
        inner_raw, conv_inner_state, parent_map, node_depth, conv_inner_weight, conv_inner_bias
    )
    heads_local = step_raw.shape[-1]
    heads_x = channels.reshape(request_count, node_count, heads_local, HEAD_DIM)
    b_part = group_values[..., :STATE]
    c_part = group_values[..., STATE:]
    step_size = jax.nn.softplus(step_raw.astype(jnp.float32) + step_bias)
    log_decay = -decay_rate * step_size
    cumulative = jnp.einsum("rij,rjh->rih", reach, log_decay, precision=HIGHEST_PRECISION)
    gap = cumulative[:, :, None, :] - cumulative[:, None, :, :]
    decays = jnp.where(reach[..., None] > 0, jnp.exp(jnp.minimum(gap, 0.0)), 0.0)
    intersection = jnp.einsum("rin,rjn->rij", c_part, b_part, precision=HIGHEST_PRECISION)
    mixing = decays * intersection[..., None] * step_size[:, None, :, :]
    output = jnp.einsum("rijh,rjhp->rihp", mixing, heads_x, precision=HIGHEST_PRECISION)
    output = output + jnp.exp(cumulative)[..., None] * jnp.einsum(
        "rin,rhpn->rihp", c_part, prior_state, precision=HIGHEST_PRECISION
    )
    output = output + skip_gain[None, None, :, None] * heads_x
    slot_ids = jnp.arange(node_count, dtype=jnp.int32)
    valid = slot_ids[None, :] < tree_size[:, None]
    output = jnp.where(valid[:, :, None, None], output, 0.0).reshape(request_count, node_count, -1)
    gated = output * jax.nn.silu(gate_raw.astype(jnp.float32))
    squares = jnp.sum(gated * gated, axis=-1)
    squares = squares + from_partner(squares, "head", 0)
    mean_square = squares / (INNER // GROUPS)
    normed = (gated * lax.rsqrt(mean_square + 1e-05)[..., None] * norm_gain).astype(jnp.bfloat16)
    mixed = finish(normed.reshape(token_rows, -1), wx, wy)
    last_pick = slot_ids[None, :] == (path_length - 1)[:, None]
    leaf_node = jnp.sum(jnp.where(last_pick, accepted_path, 0), axis=1)
    leaf_row = (slot_ids[None, :] == leaf_node[:, None]).astype(jnp.float32)
    leaf_reach = jnp.einsum("ri,rij->rj", leaf_row, reach, precision=HIGHEST_PRECISION)
    leaf_cumulative = jnp.einsum("ri,rih->rh", leaf_row, cumulative, precision=HIGHEST_PRECISION)
    leaf_gap = leaf_cumulative[:, None, :] - cumulative
    weights_leaf = (
        jnp.where(leaf_reach[..., None] > 0, jnp.exp(jnp.minimum(leaf_gap, 0.0)), 0.0) * step_size
    )
    next_state = jnp.exp(leaf_cumulative)[:, :, None, None] * prior_state
    next_state = next_state + jnp.einsum(
        "rjh,rjhp,rjn->rhpn", weights_leaf, heads_x, b_part, precision=HIGHEST_PRECISION
    )
    return (mixed, next_state)


def solution(mesh):
    in_specs = (
        P("req", "head"),
        P("req", "head", None, None),
        P("req", None, "head"),
        P("req", None, "head"),
        P("req", "head"),
        P("req", "head"),
        P("req", "head"),
        P("req", "head"),
        P(None, "head"),
        P("head"),
        P(None, "head"),
        P("head"),
        P("head"),
        P("head"),
        P("head"),
        P("head"),
        P("head", "req"),
        P("req", None),
        P("req", None),
        P("req"),
        P("req"),
    )
    out_specs = (P("req", "head"), P("req", "head", None, None))
    return jax.shard_map(
        on_device, mesh=mesh, in_specs=in_specs, out_specs=out_specs, check_vma=False
    )
```

```python
import functools

import jax
import jax.numpy as jnp
from jax import lax
from jax.experimental import pallas as pl
from jax.experimental.pallas import tpu as pltpu
from jax.sharding import PartitionSpec as P

GROUP_WIDTH = 2048
MESH = pl.DeviceIdType.MESH
F32 = jnp.float32
BF16 = jnp.bfloat16
HIGHEST = lax.Precision.HIGHEST
TREE_PRECISION = HIGHEST
UNITS = (
    ("group", 0, 128, 128),
    ("inner", 0, 512, 256),
    ("inner", 256, 768, 256),
    ("gate", 0, 512, 256),
    ("gate", 256, 768, 256),
)


class Place:
    def __init__(self):
        self.r = lax.axis_index("req")
        self.h = lax.axis_index("head")
        self.y, self.x = self.r // 4, self.r % 4
        self.z, self.c = self.h // 2, self.h % 2

    def at(self, dy=0, dx=0, dz=0, dc=0):
        y, x = (self.y + dy) % 4, (self.x + dx) % 4
        z, c = (self.z + dz) % 8, (self.c + dc) % 2
        return (y * 4 + x, z * 2 + c)


def remote(src, dst, send, recv, device):
    return pltpu.make_async_remote_copy(
        src_ref=src, dst_ref=dst, send_sem=send, recv_sem=recv,
        device_id=device, device_id_type=MESH,
    )


def meet(devices, maybe=()):
    barrier = pltpu.get_barrier_semaphore()
    for device in devices:
        pl.semaphore_signal(barrier, inc=1, device_id=device, device_id_type=MESH)
    for device, here in maybe:
        @pl.when(here)
        def _():
            pl.semaphore_signal(barrier, inc=1, device_id=device, device_id_type=MESH)
    pl.semaphore_wait(barrier, len(devices) + sum(jnp.where(here, 1, 0) for _, here in maybe))


def dot(a, b, precision=None):
    return jnp.dot(a, b, preferred_element_type=F32, precision=precision)


def dot_nt(a, b, precision=None):
    return lax.dot_general(
        a, b, (((1,), (1,)), ((), ())), preferred_element_type=F32, precision=precision
    )


def dot_tn(a, b, precision=None):
    return lax.dot_general(
        a, b, (((0,), (0,)), ((), ())), preferred_element_type=F32, precision=precision
    )


def silu(u):
    return u / (1.0 + jnp.exp(-u))


def iota(shape, axis):
    return lax.broadcasted_iota(jnp.int32, shape, axis)


class Unit:
    def __init__(self, place, first, weight, column, width, tokens, out, bufs, send, recv):
        self.p, self.first = place, first
        self.a, self.b = (place.x, place.y) if first == "x" else (place.y, place.x)
        self.weight, self.column, self.width = weight, column, width
        self.tokens, self.out = tokens, out
        (self.s1, self.rf, self.s2p, self.s2m, self.rgp, self.rgm, self.q,
         self.s3, self.rh, self.s4p, self.s4m, self.rip, self.rim) = bufs
        self.send, self.recv = send, recv
        self.copies = {}

    def along(self, which, step):
        name = self.first if which == "a" else ("y" if self.first == "x" else "x")
        return self.p.at(dy=step) if name == "y" else self.p.at(dx=step)

    def part(self, dest_a, b):
        slot = 4 * b + dest_a if self.first == "x" else 4 * dest_a + b
        return dot(
            self.tokens[slot], self.weight[:, self.column : self.column + self.width]
        )

    def put(self, k, src, dst, which, step):
        copy = remote(src, dst, self.send.at[k], self.recv.at[k], self.along(which, step))
        copy.start()
        self.copies[k] = copy

    def stage1(self):
        far = (self.a + 2) % 4

        @pl.loop(0, 4)
        def _(b):
            self.s1[b] = self.part(far, b).astype(BF16)

        self.put(0, self.s1.at[0:2], self.rf.at[0:2], "a", 1)
        self.put(1, self.s1.at[2:4], self.rf.at[2:4], "a", -1)

    def stage2(self):
        self.copies[0].wait_recv()
        self.copies[1].wait_recv()
        up, down = (self.a + 1) % 4, (self.a + 3) % 4

        @pl.loop(0, 2)
        def _(b):
            self.s2p[b] = (self.part(up, b) + self.rf[b].astype(F32)).astype(BF16)
            self.s2p[b + 2] = self.part(up, b + 2).astype(BF16)
            self.s2m[b] = self.part(down, b).astype(BF16)
            self.s2m[b + 2] = (self.part(down, b + 2) + self.rf[b + 2].astype(F32)).astype(BF16)

        self.put(2, self.s2p, self.rgp, "a", 1)
        self.put(3, self.s2m, self.rgm, "a", -1)

    def stage3(self):
        self.copies[2].wait_recv()
        self.copies[3].wait_recv()

        @pl.loop(0, 4)
        def _(b):
            self.q[b] = self.part(self.a, b) + self.rgp[b].astype(F32) + self.rgm[b].astype(F32)

        self.s3[...] = self.q[(self.b + 2) % 4].astype(BF16)
        self.put(4, self.s3.at[0:64], self.rh.at[0:64], "b", 1)
        self.put(5, self.s3.at[64:128], self.rh.at[64:128], "b", -1)

    def stage4(self):
        self.copies[4].wait_recv()
        self.copies[5].wait_recv()
        up, down = (self.b + 1) % 4, (self.b + 3) % 4
        self.s4p[0:64] = (self.q[up, 0:64] + self.rh[0:64].astype(F32)).astype(BF16)
        self.s4p[64:128] = self.q[up, 64:128].astype(BF16)
        self.s4m[0:64] = self.q[down, 0:64].astype(BF16)
        self.s4m[64:128] = (self.q[down, 64:128] + self.rh[64:128].astype(F32)).astype(BF16)
        self.put(6, self.s4p, self.rip, "b", 1)
        self.put(7, self.s4m, self.rim, "b", -1)

    def stage5(self):
        self.copies[6].wait_recv()
        self.copies[7].wait_recv()
        total = self.q[self.b] + self.rip[...].astype(F32) + self.rim[...].astype(F32)
        self.out[0:128, self.column : self.column + self.width] = total.astype(BF16)

    def finish(self):
        for copy in self.copies.values():
            copy.wait_send()


def unit_scratch(width):
    def block(n, dtype=BF16):
        return pltpu.VMEM((n, 128, width), dtype)

    flat = pltpu.VMEM((128, width), BF16)
    return [block(4)] * 6 + [block(4, F32)] + [flat] * 6


def tree_setup(parents, reach, lags, sinner, sgroup, vinner, vgroup):
    lane = iota((1, 128), 1)
    own = jnp.concatenate((parents[0:1], parents[1:2]), axis=1)
    own = jnp.where(own < 0, -1, jnp.where(lane < 64, own, own + 64))
    parent = (iota((128, 128), 0) == own).astype(F32).T
    step = parent.astype(BF16)
    covered = (iota((128, 128), 0) == iota((128, 128), 1)).astype(F32) + parent
    for _ in range(6):
        half = covered.astype(BF16)
        covered = jnp.minimum(dot(half, half), 1.0)
    reach[...] = covered
    depth = jnp.sum(covered, axis=1, keepdims=True).astype(jnp.int32) - 1
    row, col = iota((128, 128), 0), iota((128, 128), 1)
    same = (col < 6) & (row // 64 == col // 3)
    ancestor = step
    for k in range(1, 4):
        if k > 1:
            ancestor = dot(ancestor, step).astype(BF16)
        prior = same & (k > depth) & (col % 3 == 3 - k + depth)
        lags[128 * (k - 1) : 128 * k, 0:128] = ancestor
        lags[128 * (k - 1) : 128 * k, 128:256] = prior.astype(F32).astype(BF16)
    for prior, values in ((sinner, vinner), (sgroup, vgroup)):
        width = values.shape[1]
        six = jnp.concatenate((prior[0].astype(F32), prior[1].astype(F32)), axis=0)
        six = jnp.concatenate((six, jnp.zeros((2, width), F32)), axis=0)
        values[128:256] = jnp.concatenate((six, jnp.zeros((120, width), F32)), axis=0).astype(BF16)


def tree_conv(values, lags, taps, bias, lo, width):
    at = slice(lo, lo + width)
    earlier = dot(lags[...], values[:, at])
    taps = taps[:, at].astype(F32)
    total = bias + taps[3:4] * values[0:128, at].astype(F32)
    for k in range(1, 4):
        total = total + taps[3 - k : 4 - k] * earlier[128 * (k - 1) : 128 * k]
    return silu(total)


def as_column(row):
    n = row.shape[1]
    return jnp.sum(jnp.where(iota((n, n), 0) == iota((n, n), 1), row, 0.0), axis=1, keepdims=True)


def tree_steps(sums, params, reach, path, plen, sizes, cum_t, cum, leaf_w, leaf_e):
    raw = sums.astype(BF16).astype(F32) + as_column(params[3:4, 0:16])
    size = jnp.maximum(raw, 0.0) + jnp.log1p(jnp.exp(-jnp.abs(raw)))
    log_decay = -as_column(params[4:5, 0:16]) * size
    total = dot_nt(log_decay, reach[...], HIGHEST)
    sizes[...] = size
    cum_t[...] = total
    cum[...] = total.T
    weights = jnp.zeros((16, 128), F32)
    for q in range(2):
        last = iota((1, 64), 1) == plen[q] - 1
        leaf = jnp.sum(jnp.where(last, path[q : q + 1], 0), axis=1, keepdims=True) + 64 * q
        here = (iota((1, 128), 1) == leaf).astype(F32)
        above = dot(here.astype(BF16), reach[...].astype(BF16))
        at_leaf = jnp.sum(here * total, axis=1, keepdims=True)
        weights = weights + jnp.where(above > 0, jnp.exp(jnp.minimum(at_leaf - total, 0.0)), 0.0)
        leaf_e[:, 128 * q : 128 * q + 128] = jnp.broadcast_to(jnp.exp(at_leaf), (16, 128))
    leaf_w[...] = (weights * size).T


def tree_outputs(values, states, channels, sizes, cum_t, cum, reach, params, tsize, out):
    for q in range(2):
        rows = slice(64 * q, 64 * q + 64)
        out[rows] = dot_nt(values[1, rows], states[q], TREE_PRECISION)
    meet_bc = dot_nt(values[1], values[0], TREE_PRECISION)
    linked = reach[...] > 0
    lane = iota((128, 128), 1) < 64
    row = iota((128, 1), 0)
    valid = jnp.where(row < 64, row, row - 64) < jnp.where(row < 64, tsize[0], tsize[1])
    for pair in range(8):
        at = slice(128 * pair, 128 * pair + 128)
        x = channels[:, at]
        mixes, grown, skips = [], [], []
        for head in (2 * pair, 2 * pair + 1):
            column, across = cum[:, head : head + 1], cum_t[head : head + 1]
            decay = jnp.where(linked, jnp.exp(jnp.minimum(column - across, 0.0)), 0.0)
            mixes.append(decay * meet_bc * sizes[head : head + 1])
            grown.append(jnp.exp(column))
            skips.append(params[5:6, head : head + 1])
        both = dot(
            jnp.concatenate(mixes, axis=1),
            jnp.concatenate((jnp.where(lane, x, 0.0), jnp.where(lane, 0.0, x)), axis=0),
            TREE_PRECISION,
        )
        total = both + jnp.where(lane, grown[0], grown[1]) * out[:, at]
        total = total + jnp.where(lane, skips[0], skips[1]) * x
        out[:, at] = jnp.where(valid, total, 0.0)


def advance(q, part, states, channels, values, leaf_w, leaf_e):
    rows = slice(64 * q, 64 * q + 64)
    lane = iota((64, 128), 1) < 64
    for pair in range(4 * part, 4 * part + 4):
        at = slice(128 * pair, 128 * pair + 128)
        weight = jnp.where(
            lane, leaf_w[rows, 2 * pair : 2 * pair + 1], leaf_w[rows, 2 * pair + 1 : 2 * pair + 2]
        )
        added = dot_tn(channels[rows, at] * weight, values[0, rows], TREE_PRECISION)
        for j in range(2):
            head = 2 * pair + j
            kept = leaf_e[head : head + 1, 128 * q : 128 * q + 1]
            block = slice(64 * head, 64 * head + 64)
            states[q, block] = kept * states[q, block] + added[64 * j : 64 * j + 64]


ORDER = (
    (1, 0), (1, 1), (2, 0), (1, 2), (2, 1), (3, 0), (1, 3), (2, 2), (3, 1), (4, 0), (1, 4),
    (3, 2), (4, 1), (5, 0), (2, 3), (4, 2), (5, 1), (2, 4), (5, 2),
    (3, 3), (3, 4), (4, 3), (4, 4), (5, 3), (5, 4),
)


def mixer_kernel(*refs):
    (tok, state, sinner, sgroup, wgate_hbm, winner_hbm, wgroup_hbm, wstep, tinner, tgroup,
     params, wout, parents, path, plen, tsize, mixed, next_state,
     tg, st, sr, wst, wgate, winner, wgroup, states, wx, wy,
     reach, lags, vinner, vgroup, gate, values, channels, sizes, cum_t, cum, leaf_w, leaf_e,
     outs_f, sq_s, sq_r, norm,
     nx, ny, own, sent, got, zsend_p, zsend_m, zgot_p, zgot_m, fin, land,
     loads, turn_s, turn_r, local, zs, zr, cs, cr, ss, sr_sem, os, orr, gs, gr, us, ur,
     bc_s, bc_r, sq_ss, sq_rs, ns, nr, ks, kr, vs, vr, fs, fr, store) = refs[:84]
    bufs = refs[84:]
    p = Place()
    r, h, y, x, z, c = p.r, p.h, p.y, p.x, p.z, p.c
    hy, hx = h // 4, h % 4
    other = hy * 4 + hx
    moved = r != h
    goal = ((hy * 4 + x, y * 4 + hx), (y * 4 + hx, hy * 4 + x))
    away = (hy != y, hx != x)

    fetch = []
    for k, (src, dst) in enumerate(
        ((wgroup_hbm, wgroup), (winner_hbm, winner), (wgate_hbm, wgate), (state, states))
    ):
        fetch.append(pltpu.make_async_copy(src, dst, loads.at[k]))
        fetch[-1].start()

    meet(
        [((r + j) % 16, h) for j in range(1, 16)] + [p.at(dz=1), p.at(dz=-1), p.at(dc=1)],
        [((other, r), moved), (goal[0], away[0]), (goal[1], away[1])],
    )
    turn = remote(tok, tg.at[r], turn_s, turn_r, (other, r))
    keep_tok = pltpu.make_async_copy(tok, tg.at[r], local)

    @pl.when(moved)
    def _():
        turn.start()

    @pl.when(jnp.logical_not(moved))
    def _():
        keep_tok.start()

    near, keeps = [], []
    for k, (ax, full, lo, d) in enumerate(
        (("x", wx, 0, 1), ("x", wx, 0, -1), ("y", wy, 256, 1), ("y", wy, 256, -1))
    ):
        me = x if ax == "x" else y
        peer = p.at(dx=d) if ax == "x" else p.at(dy=d)
        copy = remote(wout.at[:, lo : lo + 256], full.at[me], os.at[k], orr.at[k], peer)
        copy.start()
        near.append((copy, ax, full, d, me, peer))
        if d == 1:
            keeps.append(pltpu.make_async_copy(wout.at[:, lo : lo + 256], full.at[me], loads.at[4 + k // 2]))
            keeps[-1].start()

    tree_setup(parents, reach, lags, sinner, sgroup, vinner, vgroup)
    wst[...] = wstep[...].astype(F32).T.astype(BF16)

    @pl.when(moved)
    def _():
        turn.wait()

    @pl.when(jnp.logical_not(moved))
    def _():
        keep_tok.wait()

    def block(dz):
        return 2 * ((z + dz) % 8) + c

    cores, ring = [], []

    def to_core(dz):
        k = len(cores)
        copy = remote(tg.at[block(dz)], tg.at[block(dz)], cs.at[k], cr.at[k], p.at(dc=1))
        copy.start()
        cores.append(copy)

    def hop(dz, d, lo, n):
        k = len(ring)
        ref = tg.at[block(dz), lo : lo + n]
        copy = remote(ref, ref, zs.at[k], zr.at[k], p.at(dz=d))
        copy.start()
        ring.append(copy)
        return copy

    plus, minus = hop(0, 1, 0, 128), hop(0, -1, 0, 128)
    to_core(0)
    for s in range(1, 4):
        rows = 128 if s < 3 else 64
        plus.wait_recv()
        plus = hop(-s, 1, 0, rows)
        minus.wait_recv()
        minus = hop(s, -1, 128 - rows, rows)
        to_core(-s)
        to_core(s)
    plus.wait_recv()
    minus.wait_recv()
    to_core(4)
    far = []
    for k, (copy, ax, full, d, me, peer) in enumerate(near):
        copy.wait_recv()
        lo = 0 if d == 1 else 512
        ref = full.at[(me - d) % 4, lo : lo + 512]
        far.append(remote(ref, ref, gs.at[k], gr.at[k], peer))
        far[-1].start()
    for copy in cores:
        copy.wait_recv()
    for copy in fetch[:3]:
        copy.wait()

    @pl.loop(0, 16)
    def _(k):
        st[k] = dot_nt(wst[...], tg[k])

    @pl.loop(1, 16)
    def _(j):
        to = (r + j) % 16
        remote(st.at[to], sr.at[j], ss, sr_sem, (to, h)).start()

    sources = {"group": wgroup, "inner": winner, "gate": wgate}
    results = {"group": vgroup, "inner": vinner, "gate": gate}
    units = []
    for i, (name, xcol, ycol, width) in enumerate(UNITS):
        pair = []
        for j, (first, col) in enumerate((("x", xcol), ("y", ycol))):
            n = 2 * i + j
            pair.append(Unit(p, first, sources[name], col, width, tg, results[name],
                             bufs[13 * n : 13 * n + 13], us.at[n], ur.at[n]))
        units.append(pair)
    swap = remote(values.at[c], values.at[c], bc_s, bc_r, p.at(dc=1))
    tail = sr.at[1:16]
    for stage, unit in ORDER:
        for one in units[unit]:
            getattr(one, "stage%d" % stage)()
        if (stage, unit) == (5, 0):
            values[c] = tree_conv(vgroup, lags, tgroup, params[2:3, 0:256], 0, 256)
            swap.start()
            pltpu.make_async_copy(tail, tail, sr_sem).wait()
            sums = st[r]
            for j in range(1, 16):
                sums = sums + sr[j]
            tree_steps(sums, params, reach, path, plen, sizes, cum_t, cum, leaf_w, leaf_e)
        if stage == 5 and unit in (1, 2):
            for one in units[unit]:
                lo = one.column
                channels[:, lo : lo + 256] = tree_conv(
                    vinner, lags, tinner, params[1:2, lo : lo + 256], lo, 256
                )
        if (stage, unit) == (5, 2):
            swap.wait_recv()
            fetch[3].wait()
            tree_outputs(values, states, channels, sizes, cum_t, cum, reach, params, tsize, outs_f)

    squares = jnp.zeros((128, 128), F32)
    for k in range(8):
        at = slice(128 * k, 128 * k + 128)
        gated = outs_f[:, at] * silu(gate[:, at].astype(F32))
        outs_f[:, at] = gated
        squares = squares + gated * gated
    sq_s[...] = squares
    trade = remote(sq_s, sq_r, sq_ss, sq_rs, p.at(dc=1))
    trade.start()
    trade.wait_recv()
    mean = jnp.sum(sq_s[...] + sq_r[...], axis=1, keepdims=True) / GROUP_WIDTH
    norm[...] = (outs_f[...] * lax.rsqrt(mean + 1e-05) * params[0:1]).astype(BF16)

    spread = []
    for d in (1, 3, 2):
        for full, peer in ((ny.at[y], p.at(dy=d)), (nx.at[x], p.at(dx=d))):
            k = len(spread)
            copy = remote(norm, full, ns.at[k], nr.at[k], peer)
            copy.start()
            spread.append(copy)
    nx[x] = norm[...]
    ny[y] = norm[...]
    for copy in keeps:
        copy.wait()
    for copy in far:
        copy.wait_recv()

    def shard(zz, cc):
        s = 2 * zz + cc
        i, j = s // 4, s % 4
        return dot(ny[i], wx[j]), dot(nx[j], wy[i])

    for copy in spread:
        copy.wait_recv()

    @pl.loop(0, 8)
    def _(zz):
        left, right = shard(zz, 1 - c)
        sent[zz, 0] = left.astype(BF16)
        sent[zz, 1] = right.astype(BF16)

    pass_on = remote(sent, got, ks, kr, p.at(dc=1))
    pass_on.start()

    @pl.loop(0, 8)
    def _(zz):
        left, right = shard(zz, c)
        own[zz, 0] = left
        own[zz, 1] = right

    pass_on.wait_recv()

    def mine(dz, half):
        zz = (z + dz) % 8
        return own[zz, half] + got[zz, half].astype(F32)

    moves = []

    def move(src, dst, d):
        k = len(moves)
        copy = remote(src, dst, vs.at[k], vr.at[k], p.at(dz=d))
        copy.start()
        moves.append(copy)
        return copy

    stores = []

    def grow(k):
        q, part = k // 2, k % 2
        advance(q, part, states, channels, values, leaf_w, leaf_e)
        ref = slice(512 * part, 512 * part + 512)
        copy = pltpu.make_async_copy(states.at[q, ref], next_state.at[q, ref], store.at[k])
        copy.start()
        stores.append(copy)

    zsend_p[0, 0] = mine(4, 0).astype(BF16)
    plus = move(zsend_p.at[0, 0], zgot_p.at[0, 0], 1)
    zsend_m[0, 1] = mine(4, 1).astype(BF16)
    minus = move(zsend_m.at[0, 1], zgot_m.at[0, 1], -1)
    for s in (1, 2, 3):
        grow(s - 1)
        plus.wait_recv()
        zsend_p[s, 0] = (mine(4 - s, 0) + zgot_p[s - 1, 0].astype(F32)).astype(BF16)
        if s == 1:
            zsend_p[s, 1] = mine(4 - s, 1).astype(BF16)
        else:
            zsend_p[s, 1] = (mine(4 - s, 1) + zgot_p[s - 1, 1].astype(F32)).astype(BF16)
        plus = move(zsend_p.at[s], zgot_p.at[s], 1)
        minus.wait_recv()
        if s == 1:
            zsend_m[s, 0] = mine(s - 4, 0).astype(BF16)
        else:
            zsend_m[s, 0] = (mine(s - 4, 0) + zgot_m[s - 1, 0].astype(F32)).astype(BF16)
        zsend_m[s, 1] = (mine(s - 4, 1) + zgot_m[s - 1, 1].astype(F32)).astype(BF16)
        minus = move(zsend_m.at[s], zgot_m.at[s], -1)
    grow(3)
    plus.wait_recv()
    minus.wait_recv()

    def home(half):
        return remote(fin.at[half], land.at[half], fs.at[half], fr.at[half], goal[half])

    for half in (0, 1):
        fin[half] = (
            mine(0, half) + zgot_p[3, half].astype(F32) + zgot_m[3, half].astype(F32)
        ).astype(BF16)

        @pl.when(away[half])
        def _():
            home(half).start()

        @pl.when(jnp.logical_not(away[half]))
        def _():
            land[half] = fin[half]

    for pair in units:
        for one in pair:
            one.finish()
    pltpu.make_async_copy(tail, tail, ss).wait()
    for copy in cores + ring + [one[0] for one in near] + far + [swap, trade, pass_on] + spread + moves:
        copy.wait_send()
    for copy in stores:
        copy.wait()
    for half in (0, 1):

        @pl.when(away[half])
        def _():
            home(half).wait()

        mixed[:, 256 * half : 256 * half + 256] = land[half]


def mixer(*args):
    vmem = pl.BlockSpec(memory_space=pltpu.VMEM)
    smem = pl.BlockSpec(memory_space=pltpu.SMEM)
    hbm = pl.BlockSpec(memory_space=pl.ANY)
    dma = pltpu.SemaphoreType.DMA

    def flat(*shape):
        return pltpu.VMEM(shape, F32)

    def half(*shape):
        return pltpu.VMEM(shape, BF16)

    scratch = [
        half(16, 128, 512), flat(16, 16, 128), flat(16, 16, 128), half(16, 512),
        half(512, 1024), half(512, 1024), half(512, 256), flat(2, 1024, 256),
        half(4, 1024, 256), half(4, 1024, 256),
        flat(128, 128), half(384, 256), half(256, 1024), half(256, 256), half(128, 1024),
        flat(2, 128, 256), flat(128, 1024), flat(16, 128), flat(16, 128), flat(128, 16),
        flat(128, 16), flat(16, 256), flat(128, 1024), flat(128, 128), flat(128, 128),
        half(128, 1024),
        half(4, 128, 1024), half(4, 128, 1024), flat(8, 2, 128, 256),
        half(8, 2, 128, 256), half(8, 2, 128, 256),
        half(4, 2, 128, 256), half(4, 2, 128, 256), half(4, 2, 128, 256), half(4, 2, 128, 256),
        half(2, 128, 256), half(2, 128, 256),
        dma((6,)), dma, dma, dma, dma((8,)), dma((8,)), dma((8,)), dma((8,)), dma, dma,
        dma((4,)), dma((4,)), dma((4,)), dma((4,)),
        dma((2 * len(UNITS), 8)), dma((2 * len(UNITS), 8)),
        dma, dma, dma, dma, dma((6,)), dma((6,)), dma, dma, dma((8,)), dma((8,)),
        dma((2,)), dma((2,)), dma((4,)),
    ]
    for _, _, _, width in UNITS:
        scratch += unit_scratch(width) * 2
    shape = jax.ShapeDtypeStruct
    return pl.pallas_call(
        mixer_kernel,
        name="mixer",
        out_shape=(shape((128, 512), BF16), shape((2, 1024, 256), F32)),
        in_specs=[vmem, hbm, vmem, vmem, hbm, hbm, hbm, vmem, vmem, vmem, vmem, hbm, vmem, vmem, smem, smem],
        out_specs=(vmem, hbm),
        scratch_shapes=scratch,
        compiler_params=pltpu.CompilerParams(
            collective_id=0, has_side_effects=True, vmem_limit_bytes=58 * 2**20
        ),
    )(*args)


def on_device(
    tokens, prior_state, conv_inner_state, conv_group_state, gate_weight, inner_weight,
    group_weight, step_weight, conv_inner_weight, conv_inner_bias, conv_group_weight,
    conv_group_bias, step_bias, decay_rate, skip_gain, norm_gain, out_weight, parents,
    accepted_path, path_length, tree_size,
):
    rows = (norm_gain, conv_inner_bias, conv_group_bias, step_bias, decay_rate, skip_gain)
    params = jnp.stack([jnp.pad(row.astype(F32), (0, 1024 - row.shape[0])) for row in rows])
    mixed, state = mixer(
        tokens, prior_state.reshape(2, 1024, 256), conv_inner_state, conv_group_state,
        gate_weight, inner_weight, group_weight, step_weight, conv_inner_weight,
        conv_group_weight, params, out_weight, parents, accepted_path, path_length, tree_size,
    )
    return mixed, state.reshape(prior_state.shape)


def solution(mesh):
    in_specs = (
        P("req", "head"),
        P("req", "head", None, None),
        P("req", None, "head"),
        P("req", None, "head"),
        P("req", "head"),
        P("req", "head"),
        P("req", "head"),
        P("req", "head"),
        P(None, "head"),
        P("head"),
        P(None, "head"),
        P("head"),
        P("head"),
        P("head"),
        P("head"),
        P("head"),
        P("head", "req"),
        P("req", None),
        P("req", None),
        P("req"),
        P("req"),
    )
    out_specs = (P("req", "head"), P("req", "head", None, None))
    return jax.shard_map(
        on_device, mesh=mesh, in_specs=in_specs, out_specs=out_specs, check_vma=False
    )
```

```python
import functools

import jax
import jax.numpy as jnp
from jax import lax
from jax.experimental import pallas as pl
from jax.experimental.pallas import tpu as pltpu
from jax.sharding import PartitionSpec as P

GROUP_WIDTH = 2048
MESH = pl.DeviceIdType.MESH
F32 = jnp.float32
BF16 = jnp.bfloat16
HIGHEST = lax.Precision.HIGHEST
TREE_PRECISION = HIGHEST
UNITS = (
    ("group", 0, 128, 128),
    ("inner", 0, 512, 256),
    ("inner", 256, 768, 256),
    ("gate", 0, 512, 256),
    ("gate", 256, 768, 256),
)


class Place:
    def __init__(self):
        self.r = lax.axis_index("req")
        self.h = lax.axis_index("head")
        self.y, self.x = self.r // 4, self.r % 4
        self.z, self.c = self.h // 2, self.h % 2

    def at(self, dy=0, dx=0, dz=0, dc=0):
        y, x = (self.y + dy) % 4, (self.x + dx) % 4
        z, c = (self.z + dz) % 8, (self.c + dc) % 2
        return (y * 4 + x, z * 2 + c)


def remote(src, dst, send, recv, device):
    return pltpu.make_async_remote_copy(
        src_ref=src, dst_ref=dst, send_sem=send, recv_sem=recv,
        device_id=device, device_id_type=MESH,
    )


def meet(devices, maybe=()):
    barrier = pltpu.get_barrier_semaphore()
    for device in devices:
        pl.semaphore_signal(barrier, inc=1, device_id=device, device_id_type=MESH)
    for device, here in maybe:
        @pl.when(here)
        def _():
            pl.semaphore_signal(barrier, inc=1, device_id=device, device_id_type=MESH)
    pl.semaphore_wait(barrier, len(devices) + sum(jnp.where(here, 1, 0) for _, here in maybe))


def dot(a, b, precision=None):
    return jnp.dot(a, b, preferred_element_type=F32, precision=precision)


def dot_nt(a, b, precision=None):
    return lax.dot_general(
        a, b, (((1,), (1,)), ((), ())), preferred_element_type=F32, precision=precision
    )


def dot_tn(a, b, precision=None):
    return lax.dot_general(
        a, b, (((0,), (0,)), ((), ())), preferred_element_type=F32, precision=precision
    )


def silu(u):
    return u / (1.0 + jnp.exp(-u))


def iota(shape, axis):
    return lax.broadcasted_iota(jnp.int32, shape, axis)


class Unit:
    def __init__(self, place, first, weight, column, width, tokens, out, bufs, send, recv):
        self.p, self.first = place, first
        self.a, self.b = (place.x, place.y) if first == "x" else (place.y, place.x)
        self.weight, self.column, self.width = weight, column, width
        self.tokens, self.out = tokens, out
        (self.s1, self.rf, self.s2p, self.s2m, self.rgp, self.rgm, self.q,
         self.s3, self.rh, self.s4p, self.s4m, self.rip, self.rim) = bufs
        self.send, self.recv = send, recv
        self.copies = {}

    def along(self, which, step):
        name = self.first if which == "a" else ("y" if self.first == "x" else "x")
        return self.p.at(dy=step) if name == "y" else self.p.at(dx=step)

    def part(self, dest_a):
        slots = [4 * b + dest_a if self.first == "x" else 4 * dest_a + b for b in range(4)]
        rows = jnp.concatenate([self.tokens[slot] for slot in slots], axis=0)
        return dot(rows, self.weight[:, self.column : self.column + self.width])

    def put(self, k, src, dst, which, step):
        copy = remote(src, dst, self.send.at[k], self.recv.at[k], self.along(which, step))
        copy.start()
        self.copies[k] = copy

    def stage1(self):
        far = self.part((self.a + 2) % 4).astype(BF16)
        for b in range(4):
            self.s1[b] = far[128 * b : 128 * b + 128]
        self.put(0, self.s1.at[0:2], self.rf.at[0:2], "a", 1)
        self.put(1, self.s1.at[2:4], self.rf.at[2:4], "a", -1)

    def stage2(self):
        for k, step, to, whole in ((0, 1, self.s2p, self.rgp), (1, -1, self.s2m, self.rgm)):
            terms = self.part((self.a + step) % 4)
            self.copies[k].wait_recv()
            for b in range(4):
                term = terms[128 * b : 128 * b + 128]
                if b // 2 == k:
                    term = term + self.rf[b].astype(F32)
                to[b] = term.astype(BF16)
            self.put(2 + k, to, whole, "a", step)

    def stage3(self):
        terms = self.part(self.a)
        self.copies[2].wait_recv()
        self.copies[3].wait_recv()
        for b in range(4):
            term = terms[128 * b : 128 * b + 128]
            self.q[b] = term + self.rgp[b].astype(F32) + self.rgm[b].astype(F32)
        self.s3[...] = self.q[(self.b + 2) % 4].astype(BF16)
        self.put(4, self.s3.at[0:64], self.rh.at[0:64], "b", 1)
        self.put(5, self.s3.at[64:128], self.rh.at[64:128], "b", -1)

    def stage4(self):
        self.copies[4].wait_recv()
        self.copies[5].wait_recv()
        up, down = (self.b + 1) % 4, (self.b + 3) % 4
        self.s4p[0:64] = (self.q[up, 0:64] + self.rh[0:64].astype(F32)).astype(BF16)
        self.s4p[64:128] = self.q[up, 64:128].astype(BF16)
        self.s4m[0:64] = self.q[down, 0:64].astype(BF16)
        self.s4m[64:128] = (self.q[down, 64:128] + self.rh[64:128].astype(F32)).astype(BF16)
        self.put(6, self.s4p, self.rip, "b", 1)
        self.put(7, self.s4m, self.rim, "b", -1)

    def stage5(self):
        self.copies[6].wait_recv()
        self.copies[7].wait_recv()
        total = self.q[self.b] + self.rip[...].astype(F32) + self.rim[...].astype(F32)
        self.out[0:128, self.column : self.column + self.width] = total.astype(BF16)

    def finish(self):
        for copy in self.copies.values():
            copy.wait_send()


def unit_scratch(width):
    def block(n, dtype=BF16):
        return pltpu.VMEM((n, 128, width), dtype)

    flat = pltpu.VMEM((128, width), BF16)
    return [block(4)] * 6 + [block(4, F32)] + [flat] * 6


def tree_setup(parents, reach, lags, priors):
    lane = iota((1, 128), 1)
    own = jnp.concatenate((parents[0:1], parents[1:2]), axis=1)
    own = jnp.where(own < 0, -1, jnp.where(lane < 64, own, own + 64))
    parent = (iota((128, 128), 0) == own).astype(F32).T
    step = parent.astype(BF16)
    covered = (iota((128, 128), 0) == iota((128, 128), 1)).astype(F32) + parent
    for _ in range(6):
        half = covered.astype(BF16)
        covered = jnp.minimum(dot(half, half), 1.0)
    reach[...] = covered
    depth = jnp.sum(covered, axis=1, keepdims=True).astype(jnp.int32) - 1
    row, col = iota((128, 128), 0), iota((128, 128), 1)
    same = (col < 6) & (row // 64 == col // 3)
    ancestor = step
    for k in range(1, 4):
        if k > 1:
            ancestor = dot(ancestor, step).astype(BF16)
        prior = same & (k > depth) & (col % 3 == 3 - k + depth)
        lags[128 * (k - 1) : 128 * k, 0:128] = ancestor
        lags[128 * (k - 1) : 128 * k, 128:256] = prior.astype(F32).astype(BF16)
    for prior, values in priors:
        width = values.shape[1]
        both = [prior[k].astype(F32) for k in range(3)]
        six = [both[k][q : q + 1] for q in range(2) for k in range(3)]
        six = jnp.concatenate(six + [jnp.zeros((2, width), F32)], axis=0)
        values[128:256] = jnp.concatenate((six, jnp.zeros((120, width), F32)), axis=0).astype(BF16)


def tree_conv(values, lags, taps, bias, lo, width):
    at = slice(lo, lo + width)
    earlier = dot(lags[...], values[:, at])
    taps = taps[:, at].astype(F32)
    total = bias + taps[3:4] * values[0:128, at].astype(F32)
    for k in range(1, 4):
        total = total + taps[3 - k : 4 - k] * earlier[128 * (k - 1) : 128 * k]
    return silu(total)


def as_column(row):
    n = row.shape[1]
    return jnp.sum(jnp.where(iota((n, n), 0) == iota((n, n), 1), row, 0.0), axis=1, keepdims=True)


def tree_steps(sums, bias, rate, reach, path, plen, sizes, cum_t, cum, leaf_w, leaf_e):
    raw = sums.astype(BF16).astype(F32) + as_column(bias[...])
    size = jnp.maximum(raw, 0.0) + jnp.log1p(jnp.exp(-jnp.abs(raw)))
    log_decay = -as_column(rate[...]) * size
    total = dot_nt(log_decay, reach[...], HIGHEST)
    sizes[...] = size
    cum_t[...] = total
    cum[...] = total.T
    weights = jnp.zeros((16, 128), F32)
    for q in range(2):
        last = iota((1, 64), 1) == plen[q] - 1
        leaf = jnp.sum(jnp.where(last, path[q : q + 1], 0), axis=1, keepdims=True) + 64 * q
        here = (iota((1, 128), 1) == leaf).astype(F32)
        above = dot(here.astype(BF16), reach[...].astype(BF16))
        at_leaf = jnp.sum(here * total, axis=1, keepdims=True)
        weights = weights + jnp.where(above > 0, jnp.exp(jnp.minimum(at_leaf - total, 0.0)), 0.0)
        leaf_e[:, 128 * q : 128 * q + 128] = jnp.broadcast_to(jnp.exp(at_leaf), (16, 128))
    leaf_w[...] = (weights * size).T


def tree_outputs(values, states, channels, sizes, cum_t, cum, reach, gain, tsize, out):
    for q in range(2):
        rows = slice(64 * q, 64 * q + 64)
        out[rows] = dot_nt(values[1, rows], states[q], TREE_PRECISION)
    meet_bc = dot_nt(values[1], values[0], TREE_PRECISION)
    linked = reach[...] > 0
    lane = iota((128, 128), 1) < 64
    row = iota((128, 1), 0)
    valid = jnp.where(row < 64, row, row - 64) < jnp.where(row < 64, tsize[0], tsize[1])
    for pair in range(8):
        at = slice(128 * pair, 128 * pair + 128)
        x = channels[:, at]
        mixes, grown, skips = [], [], []
        for head in (2 * pair, 2 * pair + 1):
            column, across = cum[:, head : head + 1], cum_t[head : head + 1]
            decay = jnp.where(linked, jnp.exp(jnp.minimum(column - across, 0.0)), 0.0)
            mixes.append(decay * meet_bc * sizes[head : head + 1])
            grown.append(jnp.exp(column))
            skips.append(gain[0:1, head : head + 1])
        both = dot(
            jnp.concatenate(mixes, axis=1),
            jnp.concatenate((jnp.where(lane, x, 0.0), jnp.where(lane, 0.0, x)), axis=0),
            TREE_PRECISION,
        )
        total = both + jnp.where(lane, grown[0], grown[1]) * out[:, at]
        total = total + jnp.where(lane, skips[0], skips[1]) * x
        out[:, at] = jnp.where(valid, total, 0.0)


def advance(q, part, states, channels, values, leaf_w, leaf_e):
    rows = slice(64 * q, 64 * q + 64)
    lane = iota((64, 128), 1) < 64
    for pair in range(4 * part, 4 * part + 4):
        at = slice(128 * pair, 128 * pair + 128)
        weight = jnp.where(
            lane, leaf_w[rows, 2 * pair : 2 * pair + 1], leaf_w[rows, 2 * pair + 1 : 2 * pair + 2]
        )
        added = dot_tn(channels[rows, at] * weight, values[0, rows], TREE_PRECISION)
        for j in range(2):
            head = 2 * pair + j
            kept = leaf_e[head : head + 1, 128 * q : 128 * q + 1]
            block = slice(64 * head, 64 * head + 64)
            states[q, block] = kept * states[q, block] + added[64 * j : 64 * j + 64]


ORDER = (
    (1, 0), (1, 1), (2, 0), (1, 2), (2, 1), (3, 0), (1, 3), (2, 2), (3, 1), (4, 0), (1, 4),
    (3, 2), (4, 1), (5, 0), (2, 3), (4, 2), (5, 1), (2, 4), (5, 2),
    (3, 3), (3, 4), (4, 3), (4, 4), (5, 3), (5, 4),
)


def mixer_kernel(*refs):
    (tok, state, sinner, sgroup, wgate_hbm, winner_hbm, wgroup_hbm, wst, tinner, tgroup,
     biases, step_bias, decay_rate, skip_gain, norm_gain, wout, parents, path, plen, tsize,
     mixed, next_state,
     tg, st, sr, wgate, winner, wgroup, states, wx, wy,
     reach, lags, vinner, vgroup, gate, values, channels, sizes, cum_t, cum, leaf_w, leaf_e,
     outs_f, sq_s, sq_r, inv, inv_x, inv_y, norm,
     nx, ny, own, sent, got, zsend_p, zsend_m, zgot_p, zgot_m, fin, land,
     loads, turn_s, turn_r, local, zs, zr, cs, cr, ss, sr_sem, os, orr, gs, gr, us, ur,
     bc_s, bc_r, sq_ss, sq_rs, is_, ir, ns, nr, ks, kr, vs, vr, fs, fr, store) = refs[:92]
    bufs = refs[92:]
    p = Place()
    r, h, y, x, z, c = p.r, p.h, p.y, p.x, p.z, p.c
    hy, hx = h // 4, h % 4
    turn_to = (h, 2 * ((z + r // 2) % 8) + r % 2)
    turn_from = (2 * ((z - r // 2) % 8) + c, r)
    moved = jnp.logical_or(turn_to[0] != r, turn_to[1] != h)
    goal = ((hy * 4 + x, y * 4 + hx), (y * 4 + hx, hy * 4 + x))
    away = (hy != y, hx != x)

    fetch = []
    for k, (src, dst) in enumerate(
        ((wgroup_hbm, wgroup), (winner_hbm, winner), (wgate_hbm, wgate), (state, states))
    ):
        fetch.append(pltpu.make_async_copy(src, dst, loads.at[k]))
        fetch[-1].start()

    meet(
        [((r + j) % 16, h) for j in range(1, 16)] + [p.at(dz=1), p.at(dz=-1), p.at(dc=1)],
        [(turn_from, moved), (goal[0], away[0]), (goal[1], away[1])],
    )
    turn = remote(tok, tg.at[r], turn_s, turn_r, turn_to)
    keep_tok = pltpu.make_async_copy(tok, tg.at[r], local)

    @pl.when(moved)
    def _():
        turn.start()

    @pl.when(jnp.logical_not(moved))
    def _():
        keep_tok.start()

    tree_setup(parents, reach, lags, ((sinner, vinner), (sgroup, vgroup)))

    @pl.when(moved)
    def _():
        turn.wait()

    @pl.when(jnp.logical_not(moved))
    def _():
        keep_tok.wait()

    near, keeps = [], []
    for k, (ax, full, lo, d) in enumerate(
        (("x", wx, 0, 1), ("x", wx, 0, -1), ("y", wy, 256, 1), ("y", wy, 256, -1))
    ):
        me = x if ax == "x" else y
        peer = p.at(dx=d) if ax == "x" else p.at(dy=d)
        first = 0 if d == 1 else 512
        for n, rows in enumerate((first, 512 - first)):
            copy = remote(
                wout.at[rows : rows + 512, lo : lo + 256], full.at[me, rows : rows + 512],
                os.at[2 * k + n], orr.at[2 * k + n], peer,
            )
            copy.start()
            near.append((copy, ax, full, d, me, peer))
        if d == 1:
            keeps.append(pltpu.make_async_copy(wout.at[:, lo : lo + 256], full.at[me], loads.at[4 + k // 2]))
            keeps[-1].start()

    def block(dz):
        return 2 * ((z + dz - r // 2) % 8) + c

    cores, ring, far = [], {}, []

    def to_core(dz):
        k = len(cores)
        copy = remote(tg.at[block(dz)], tg.at[block(dz)], cs.at[k], cr.at[k], p.at(dc=1))
        copy.start()
        cores.append(copy)

    def hop(d, s, i):
        k = (d > 0) * 16 + s * 4 + i
        ref = tg.at[block(-s * d), 32 * i : 32 * i + 32]
        ring[d, s, i] = remote(ref, ref, zs.at[k], zr.at[k], p.at(dz=d))
        ring[d, s, i].start()

    for s in range(4):
        for i in range(4):
            for d in (1, -1):
                if s > 0:
                    ring[d, s - 1, i].wait_recv()
                if s < 3 or (d == 1) == (i < 2):
                    hop(d, s, i)
        to_core(-s)
        if s > 0:
            to_core(s)
        if s == 2:
            for k, (copy, ax, full, d, me, peer) in enumerate(near[0::2]):
                copy.wait_recv()
                lo = 0 if d == 1 else 512
                ref = full.at[(me - d) % 4, lo : lo + 512]
                far.append(remote(ref, ref, gs.at[k], gr.at[k], peer))
                far[-1].start()
    for i in range(4):
        ring[1 if i < 2 else -1, 3, i].wait_recv()
    to_core(4)
    for copy in cores:
        copy.wait_recv()
    for copy in fetch[:3]:
        copy.wait()

    sources = {"group": wgroup, "inner": winner, "gate": wgate}
    results = {"group": vgroup, "inner": vinner, "gate": gate}
    units = []
    for i, (name, xcol, ycol, width) in enumerate(UNITS):
        pair = []
        for j, (first, col) in enumerate((("x", xcol), ("y", ycol))):
            n = 2 * i + j
            pair.append(Unit(p, first, sources[name], col, width, tg, results[name],
                             bufs[13 * n : 13 * n + 13], us.at[n], ur.at[n]))
        units.append(pair)
    swap = remote(values.at[c], values.at[c], bc_s, bc_r, p.at(dc=1))
    tail = sr.at[1:16]
    spread = []

    def part_of_norm(k):
        at = slice(256 * k, 256 * k + 256)
        gated = outs_f[:, at] * silu(gate[:, at].astype(F32))
        norm[k] = (gated * norm_gain[0:1, at]).astype(BF16)
        for d in (1, 3, 2):
            for full, peer in ((ny.at[y, k], p.at(dy=d)), (nx.at[x, k], p.at(dx=d))):
                n = len(spread)
                copy = remote(norm.at[k], full, ns.at[n], nr.at[n], peer)
                copy.start()
                spread.append(copy)
        nx[x, k] = norm[k]
        ny[y, k] = norm[k]
        return gated[:, 0:128] * gated[:, 0:128] + gated[:, 128:256] * gated[:, 128:256]

    squares = jnp.zeros((128, 128), F32)
    for stage, unit in ORDER:
        for one in units[unit]:
            getattr(one, "stage%d" % stage)()
        if (stage, unit) == (3, 0):
            @pl.loop(0, 4)
            def _(k):
                rows = jnp.concatenate([tg[4 * k + b] for b in range(4)], axis=0)
                raw = dot_nt(rows, wst[...])
                for b in range(4):
                    st[4 * k + b] = raw[128 * b : 128 * b + 128].T

            @pl.loop(1, 16)
            def _(j):
                to = (r + j) % 16
                remote(st.at[to], sr.at[j], ss, sr_sem, (to, h)).start()

        if stage == 5 and unit in (3, 4):
            for one in units[unit]:
                squares = squares + part_of_norm(one.column // 256)
        if (stage, unit) == (5, 0):
            values[c] = tree_conv(vgroup, lags, tgroup, biases[0:1, 1024:1280], 0, 256)
            swap.start()
            pltpu.make_async_copy(tail, tail, sr_sem).wait()
            sums = st[r]
            for j in range(1, 16):
                sums = sums + sr[j]
            tree_steps(sums, step_bias, decay_rate, reach, path, plen, sizes, cum_t, cum, leaf_w, leaf_e)
        if stage == 5 and unit in (1, 2):
            for one in units[unit]:
                lo = one.column
                channels[:, lo : lo + 256] = tree_conv(
                    vinner, lags, tinner, biases[0:1, lo : lo + 256], lo, 256
                )
        if (stage, unit) == (5, 2):
            swap.wait_recv()
            fetch[3].wait()
            tree_outputs(values, states, channels, sizes, cum_t, cum, reach, skip_gain, tsize, outs_f)

    sq_s[...] = jnp.broadcast_to(jnp.sum(squares.T, axis=0, keepdims=True), (8, 128))
    trade = remote(sq_s, sq_r, sq_ss, sq_rs, p.at(dc=1))
    trade.start()
    trade.wait_recv()
    inv[...] = lax.rsqrt((sq_s[...] + sq_r[...]) / GROUP_WIDTH + 1e-05)
    rates = []
    for d in (1, 3, 2):
        for full, peer in ((inv_y.at[y], p.at(dy=d)), (inv_x.at[x], p.at(dx=d))):
            n = len(rates)
            copy = remote(inv, full, is_.at[n], ir.at[n], peer)
            copy.start()
            rates.append(copy)
    inv_x[x] = inv[...]
    inv_y[y] = inv[...]
    for copy in keeps:
        copy.wait()
    for copy in far + [one[0] for one in near[1::2]] + spread + rates:
        copy.wait_recv()

    def shard(dz, cc, half):
        s = 2 * ((z + dz) % 8) + cc
        i, j = s // 4, s % 4
        rows, scale, weight = ((ny, inv_y, wx), (nx, inv_x, wy))[half]
        a, b = (i, j) if half == 0 else (j, i)
        total = dot(rows[a, 0], weight[b, 0:256])
        for k in range(1, 4):
            total = total + dot(rows[a, k], weight[b, 256 * k : 256 * k + 256])
        return total * scale[a].T[:, 0:1]

    passed = {}

    def give(dz):
        k = dz % 8
        for half in (0, 1):
            sent[k, half] = shard(dz, 1 - c, half).astype(BF16)
        passed[k] = remote(sent.at[k], got.at[k], ks.at[k], kr.at[k], p.at(dc=1))
        passed[k].start()

    def keep(dz):
        k = dz % 8
        for half in (0, 1):
            own[k, half] = shard(dz, c, half)

    def add(dz):
        k = dz % 8
        passed[k].wait_recv()
        for half in (0, 1):
            own[k, half] = own[k, half] + got[k, half].astype(F32)

    moves = []

    def move(src, dst, d):
        k = len(moves)
        copy = remote(src, dst, vs.at[k], vr.at[k], p.at(dz=d))
        copy.start()
        moves.append(copy)
        return copy

    stores = []

    def grow(k):
        q, part = k // 2, k % 2
        advance(q, part, states, channels, values, leaf_w, leaf_e)
        ref = slice(512 * part, 512 * part + 512)
        copy = pltpu.make_async_copy(states.at[q, ref], next_state.at[q, ref], store.at[k])
        copy.start()
        stores.append(copy)

    sends, gots = {1: zsend_p, -1: zsend_m}, {1: zgot_p, -1: zgot_m}
    chain = {}

    def step(d, s, half, fresh):
        k = (d * (4 - s)) % 8
        total = own[k, half]
        if not fresh:
            chain[d, half].wait_recv()
            total = total + gots[d][s - 1, half].astype(F32)
        sends[d][s, half] = total.astype(BF16)
        chain[d, half] = move(sends[d].at[s, half], gots[d].at[s, half], d)

    give(4)
    give(3)
    give(-3)
    keep(4)
    keep(3)
    keep(-3)
    add(4)
    step(1, 0, 0, True)
    step(-1, 0, 1, True)
    add(3)
    step(1, 1, 1, True)
    add(-3)
    step(-1, 1, 0, True)
    give(2)
    give(-2)
    keep(2)
    keep(-2)
    step(1, 1, 0, False)
    step(-1, 1, 1, False)
    add(2)
    add(-2)
    step(1, 2, 1, False)
    step(-1, 2, 0, False)
    give(1)
    give(-1)
    give(0)
    keep(1)
    keep(-1)
    step(1, 2, 0, False)
    step(-1, 2, 1, False)
    add(1)
    add(-1)
    step(1, 3, 1, False)
    step(-1, 3, 0, False)
    keep(0)
    grow(0)
    step(1, 3, 0, False)
    step(-1, 3, 1, False)
    add(0)
    grow(1)

    def home(half):
        return remote(fin.at[half], land.at[half], fs.at[half], fr.at[half], goal[half])

    for half in (0, 1):
        chain[1, half].wait_recv()
        chain[-1, half].wait_recv()
        fin[half] = (
            own[0, half] + zgot_p[3, half].astype(F32) + zgot_m[3, half].astype(F32)
        ).astype(BF16)

        @pl.when(away[half])
        def _():
            home(half).start()

        @pl.when(jnp.logical_not(away[half]))
        def _():
            land[half] = fin[half]

    grow(2)
    grow(3)
    for pair in units:
        for one in pair:
            one.finish()
    pltpu.make_async_copy(tail, tail, ss).wait()
    for copy in cores + list(ring.values()) + [one[0] for one in near] + far + [swap, trade]:
        copy.wait_send()
    for copy in spread + rates + list(passed.values()) + moves:
        copy.wait_send()
    for copy in stores:
        copy.wait()
    for half in (0, 1):

        @pl.when(away[half])
        def _():
            home(half).wait()

        mixed[:, 256 * half : 256 * half + 256] = land[half]


def mixer(*args):
    vmem = pl.BlockSpec(memory_space=pltpu.VMEM)
    smem = pl.BlockSpec(memory_space=pltpu.SMEM)
    hbm = pl.BlockSpec(memory_space=pl.ANY)
    dma = pltpu.SemaphoreType.DMA

    def flat(*shape):
        return pltpu.VMEM(shape, F32)

    def half(*shape):
        return pltpu.VMEM(shape, BF16)

    scratch = [
        half(16, 128, 512), flat(16, 16, 128), flat(16, 16, 128),
        half(512, 1024), half(512, 1024), half(512, 256), flat(2, 1024, 256),
        half(4, 1024, 256), half(4, 1024, 256),
        flat(128, 128), half(384, 256), half(256, 1024), half(256, 256), half(128, 1024),
        flat(2, 128, 256), flat(128, 1024), flat(16, 128), flat(16, 128), flat(128, 16),
        flat(128, 16), flat(16, 256), flat(128, 1024), flat(8, 128), flat(8, 128),
        flat(8, 128), flat(4, 8, 128), flat(4, 8, 128), half(4, 128, 256),
        half(4, 4, 128, 256), half(4, 4, 128, 256), flat(8, 2, 128, 256),
        half(8, 2, 128, 256), half(8, 2, 128, 256),
        half(4, 2, 128, 256), half(4, 2, 128, 256), half(4, 2, 128, 256), half(4, 2, 128, 256),
        half(2, 128, 256), half(2, 128, 256),
        dma((6,)), dma, dma, dma, dma((32,)), dma((32,)), dma((8,)), dma((8,)), dma, dma,
        dma((8,)), dma((8,)), dma((4,)), dma((4,)),
        dma((2 * len(UNITS), 8)), dma((2 * len(UNITS), 8)),
        dma, dma, dma, dma, dma((6,)), dma((6,)), dma((24,)), dma((24,)), dma((8,)), dma((8,)),
        dma((14,)), dma((14,)), dma((2,)), dma((2,)), dma((4,)),
    ]
    for _, _, _, width in UNITS:
        scratch += unit_scratch(width) * 2
    shape = jax.ShapeDtypeStruct
    return pl.pallas_call(
        mixer_kernel,
        name="mixer",
        out_shape=(shape((128, 512), BF16), shape((2, 1024, 256), F32)),
        in_specs=[vmem, hbm, vmem, vmem, hbm, hbm, hbm] + [vmem] * 8 + [hbm, vmem, vmem, smem, smem],
        out_specs=(vmem, hbm),
        scratch_shapes=scratch,
        compiler_params=pltpu.CompilerParams(
            collective_id=0, has_side_effects=True, vmem_limit_bytes=58 * 2**20
        ),
    )(*args)


def on_device(
    tokens, prior_state, conv_inner_state, conv_group_state, gate_weight, inner_weight,
    group_weight, step_weight, conv_inner_weight, conv_inner_bias, conv_group_weight,
    conv_group_bias, step_bias, decay_rate, skip_gain, norm_gain, out_weight, parents,
    accepted_path, path_length, tree_size,
):
    def row(vector):
        return vector.reshape(1, -1)

    mixed, state = mixer(
        tokens, prior_state.reshape(2, 1024, 256), conv_inner_state.swapaxes(0, 1),
        conv_group_state.swapaxes(0, 1), gate_weight, inner_weight, group_weight, step_weight.T,
        conv_inner_weight, conv_group_weight,
        row(lax.optimization_barrier(
            jnp.concatenate((conv_inner_bias.astype(F32), conv_group_bias.astype(F32)))
        )),
        row(step_bias), row(decay_rate), row(skip_gain), row(norm_gain), out_weight, parents,
        accepted_path, path_length, tree_size,
    )
    return mixed, state.reshape(prior_state.shape)


def solution(mesh):
    in_specs = (
        P("req", "head"),
        P("req", "head", None, None),
        P("req", None, "head"),
        P("req", None, "head"),
        P("req", "head"),
        P("req", "head"),
        P("req", "head"),
        P("req", "head"),
        P(None, "head"),
        P("head"),
        P(None, "head"),
        P("head"),
        P("head"),
        P("head"),
        P("head"),
        P("head"),
        P("head", "req"),
        P("req", None),
        P("req", None),
        P("req"),
        P("req"),
    )
    out_specs = (P("req", "head"), P("req", "head", None, None))
    return jax.shard_map(
        on_device, mesh=mesh, in_specs=in_specs, out_specs=out_specs, check_vma=False
    )
```

```python
import functools

import jax
import jax.numpy as jnp
from jax import lax
from jax.experimental import pallas as pl
from jax.experimental.pallas import tpu as pltpu
from jax.sharding import PartitionSpec as P

GROUP_WIDTH = 2048
MESH = pl.DeviceIdType.MESH
F32 = jnp.float32
BF16 = jnp.bfloat16
HIGHEST = lax.Precision.HIGHEST
TREE_PRECISION = HIGHEST
UNITS = (
    ("group", 0, 128, 128),
    ("inner", 0, 512, 256),
    ("inner", 256, 768, 256),
    ("gate", 0, 512, 256),
    ("gate", 256, 768, 256),
)


class Place:
    def __init__(self):
        self.r = lax.axis_index("req")
        self.h = lax.axis_index("head")
        self.y, self.x = self.r // 4, self.r % 4
        self.z, self.c = self.h // 2, self.h % 2

    def at(self, dy=0, dx=0, dz=0, dc=0):
        y, x = (self.y + dy) % 4, (self.x + dx) % 4
        z, c = (self.z + dz) % 8, (self.c + dc) % 2
        return (y * 4 + x, z * 2 + c)


def remote(src, dst, send, recv, device):
    return pltpu.make_async_remote_copy(
        src_ref=src, dst_ref=dst, send_sem=send, recv_sem=recv,
        device_id=device, device_id_type=MESH,
    )


def meet(devices, maybe=()):
    barrier = pltpu.get_barrier_semaphore()
    for device in devices:
        pl.semaphore_signal(barrier, inc=1, device_id=device, device_id_type=MESH)
    for device, here in maybe:
        @pl.when(here)
        def _():
            pl.semaphore_signal(barrier, inc=1, device_id=device, device_id_type=MESH)
    pl.semaphore_wait(barrier, len(devices) + sum(jnp.where(here, 1, 0) for _, here in maybe))


def dot(a, b, precision=None):
    return jnp.dot(a, b, preferred_element_type=F32, precision=precision)


def dot_nt(a, b, precision=None):
    return lax.dot_general(
        a, b, (((1,), (1,)), ((), ())), preferred_element_type=F32, precision=precision
    )


def dot_tn(a, b, precision=None):
    return lax.dot_general(
        a, b, (((0,), (0,)), ((), ())), preferred_element_type=F32, precision=precision
    )


def silu(u):
    return u / (1.0 + jnp.exp(-u))


def iota(shape, axis):
    return lax.broadcasted_iota(jnp.int32, shape, axis)


class Gather:
    def __init__(self, place, axis, block, full, rows, sems):
        self.p, self.axis, self.block, self.full, self.rows = place, axis, block, full, rows
        self.me = place.x if axis == "x" else place.y
        self.near_s, self.near_r, self.far_s, self.far_r, self.own = sems
        self.near, self.far = [], []

    def peer(self, d):
        return self.p.at(dx=d) if self.axis == "x" else self.p.at(dy=d)

    def halves(self, d):
        half = self.rows // 2
        first = 0 if d == 1 else half
        return pl.ds(first, half), pl.ds(half - first, half)

    def start(self):
        for n in range(2):
            for i, d in enumerate((1, -1)):
                rows, k = self.halves(d)[n], 2 * n + i
                self.near.append(remote(
                    self.block.at[rows], self.full.at[self.me, rows],
                    self.near_s.at[k], self.near_r.at[k], self.peer(d),
                ))
                self.near[-1].start()
        self.keep = pltpu.make_async_copy(self.block, self.full.at[self.me], self.own)
        self.keep.start()

    def forward(self):
        for i, d in enumerate((1, -1)):
            self.near[i].wait_recv()
            ref = self.full.at[(self.me - d) % 4, self.halves(d)[0]]
            self.far.append(remote(ref, ref, self.far_s.at[i], self.far_r.at[i], self.peer(d)))
            self.far[-1].start()

    def ready(self):
        self.keep.wait()
        for copy in self.near[2:] + self.far:
            copy.wait_recv()

    def finish(self):
        for copy in self.near + self.far:
            copy.wait_send()


class Unit:
    def __init__(self, place, along, gather, column, width, tokens, out, bufs, send, recv):
        self.p, self.along = place, along
        self.b = place.y if along == "y" else place.x
        self.gather, self.column, self.width = gather, column, width
        self.tokens, self.out = tokens, out
        self.q, self.s3, self.rh, self.s4p, self.s4m, self.rip, self.rim = bufs
        self.send, self.recv = send, recv
        self.copies = {}

    def put(self, k, src, dst, step):
        peer = self.p.at(dy=step) if self.along == "y" else self.p.at(dx=step)
        copy = remote(src, dst, self.send.at[k], self.recv.at[k], peer)
        copy.start()
        self.copies[k] = copy

    def stage1(self):
        self.gather.ready()
        total = None
        for k in range(4):
            rows = jnp.concatenate([self.tokens[b, k] for b in range(4)], axis=0)
            term = dot(rows, self.gather.full[k])
            total = term if total is None else total + term
        for b in range(4):
            self.q[b] = total[128 * b : 128 * b + 128]
        self.s3[...] = self.q[(self.b + 2) % 4].astype(BF16)
        self.put(0, self.s3.at[0:64], self.rh.at[0:64], 1)
        self.put(1, self.s3.at[64:128], self.rh.at[64:128], -1)

    def stage2(self):
        self.copies[0].wait_recv()
        self.copies[1].wait_recv()
        up, down = (self.b + 1) % 4, (self.b + 3) % 4
        self.s4p[0:64] = (self.q[up, 0:64] + self.rh[0:64].astype(F32)).astype(BF16)
        self.s4p[64:128] = self.q[up, 64:128].astype(BF16)
        self.s4m[0:64] = self.q[down, 0:64].astype(BF16)
        self.s4m[64:128] = (self.q[down, 64:128] + self.rh[64:128].astype(F32)).astype(BF16)
        self.put(2, self.s4p, self.rip, 1)
        self.put(3, self.s4m, self.rim, -1)

    def stage3(self):
        self.copies[2].wait_recv()
        self.copies[3].wait_recv()
        total = self.q[self.b] + self.rip[...].astype(F32) + self.rim[...].astype(F32)
        self.out[0:128, self.column : self.column + self.width] = total.astype(BF16)

    def finish(self):
        for copy in self.copies.values():
            copy.wait_send()


def unit_scratch(width):
    flat = pltpu.VMEM((128, width), BF16)
    return [pltpu.VMEM((4, 128, width), F32)] + [flat] * 6


def tree_setup(parents, reach, lags, priors):
    lane = iota((1, 128), 1)
    own = jnp.concatenate((parents[0:1], parents[1:2]), axis=1)
    own = jnp.where(own < 0, -1, jnp.where(lane < 64, own, own + 64))
    parent = (iota((128, 128), 0) == own).astype(F32).T
    step = parent.astype(BF16)
    covered = (iota((128, 128), 0) == iota((128, 128), 1)).astype(F32) + parent
    for _ in range(6):
        half = covered.astype(BF16)
        covered = jnp.minimum(dot(half, half), 1.0)
    reach[...] = covered
    depth = jnp.sum(covered, axis=1, keepdims=True).astype(jnp.int32) - 1
    row, col = iota((128, 128), 0), iota((128, 128), 1)
    same = (col < 6) & (row // 64 == col // 3)
    ancestor = step
    for k in range(1, 4):
        if k > 1:
            ancestor = dot(ancestor, step).astype(BF16)
        prior = same & (k > depth) & (col % 3 == 3 - k + depth)
        lags[128 * (k - 1) : 128 * k, 0:128] = ancestor
        lags[128 * (k - 1) : 128 * k, 128:256] = prior.astype(F32).astype(BF16)
    for prior, values in priors:
        width = values.shape[1]
        both = [prior[k].astype(F32) for k in range(3)]
        six = [both[k][q : q + 1] for q in range(2) for k in range(3)]
        six = jnp.concatenate(six + [jnp.zeros((2, width), F32)], axis=0)
        values[128:256] = jnp.concatenate((six, jnp.zeros((120, width), F32)), axis=0).astype(BF16)


def tree_conv(values, lags, taps, bias, lo, width):
    at = slice(lo, lo + width)
    earlier = dot(lags[...], values[:, at])
    taps = taps[:, at].astype(F32)
    total = bias + taps[3:4] * values[0:128, at].astype(F32)
    for k in range(1, 4):
        total = total + taps[3 - k : 4 - k] * earlier[128 * (k - 1) : 128 * k]
    return silu(total)


def as_column(row):
    n = row.shape[1]
    return jnp.sum(jnp.where(iota((n, n), 0) == iota((n, n), 1), row, 0.0), axis=1, keepdims=True)


def tree_steps(sums, bias, rate, reach, path, plen, sizes, cum_t, cum, leaf_w, leaf_e):
    raw = sums.astype(BF16).astype(F32) + as_column(bias[...])
    size = jnp.maximum(raw, 0.0) + jnp.log1p(jnp.exp(-jnp.abs(raw)))
    log_decay = -as_column(rate[...]) * size
    total = dot_nt(log_decay, reach[...], HIGHEST)
    sizes[...] = size
    cum_t[...] = total
    cum[...] = total.T
    weights = jnp.zeros((16, 128), F32)
    for q in range(2):
        last = iota((1, 64), 1) == plen[q] - 1
        leaf = jnp.sum(jnp.where(last, path[q : q + 1], 0), axis=1, keepdims=True) + 64 * q
        here = (iota((1, 128), 1) == leaf).astype(F32)
        above = dot(here.astype(BF16), reach[...].astype(BF16))
        at_leaf = jnp.sum(here * total, axis=1, keepdims=True)
        weights = weights + jnp.where(above > 0, jnp.exp(jnp.minimum(at_leaf - total, 0.0)), 0.0)
        leaf_e[:, 128 * q : 128 * q + 128] = jnp.broadcast_to(jnp.exp(at_leaf), (16, 128))
    leaf_w[...] = (weights * size).T


def tree_outputs(values, states, channels, sizes, cum_t, cum, reach, gain, tsize, out):
    for q in range(2):
        rows = slice(64 * q, 64 * q + 64)
        out[rows] = dot_nt(values[1, rows], states[q], TREE_PRECISION)
    meet_bc = dot_nt(values[1], values[0], TREE_PRECISION)
    linked = reach[...] > 0
    lane = iota((128, 128), 1) < 64
    row = iota((128, 1), 0)
    valid = jnp.where(row < 64, row, row - 64) < jnp.where(row < 64, tsize[0], tsize[1])
    for pair in range(8):
        at = slice(128 * pair, 128 * pair + 128)
        x = channels[:, at]
        mixes, grown, skips = [], [], []
        for head in (2 * pair, 2 * pair + 1):
            column, across = cum[:, head : head + 1], cum_t[head : head + 1]
            decay = jnp.where(linked, jnp.exp(jnp.minimum(column - across, 0.0)), 0.0)
            mixes.append(decay * meet_bc * sizes[head : head + 1])
            grown.append(jnp.exp(column))
            skips.append(gain[0:1, head : head + 1])
        both = dot(
            jnp.concatenate(mixes, axis=1),
            jnp.concatenate((jnp.where(lane, x, 0.0), jnp.where(lane, 0.0, x)), axis=0),
            TREE_PRECISION,
        )
        total = both + jnp.where(lane, grown[0], grown[1]) * out[:, at]
        total = total + jnp.where(lane, skips[0], skips[1]) * x
        out[:, at] = jnp.where(valid, total, 0.0)


def advance(q, part, states, channels, values, leaf_w, leaf_e):
    rows = slice(64 * q, 64 * q + 64)
    lane = iota((64, 128), 1) < 64
    for pair in range(4 * part, 4 * part + 4):
        at = slice(128 * pair, 128 * pair + 128)
        weight = jnp.where(
            lane, leaf_w[rows, 2 * pair : 2 * pair + 1], leaf_w[rows, 2 * pair + 1 : 2 * pair + 2]
        )
        added = dot_tn(channels[rows, at] * weight, values[0, rows], TREE_PRECISION)
        for j in range(2):
            head = 2 * pair + j
            kept = leaf_e[head : head + 1, 128 * q : 128 * q + 1]
            block = slice(64 * head, 64 * head + 64)
            states[q, block] = kept * states[q, block] + added[64 * j : 64 * j + 64]


ORDER = (
    (1, 0), (1, 1), (1, 2), (2, 0), (1, 3), (2, 1), (3, 0), (1, 4), (2, 2), (3, 1),
    (2, 3), (3, 2), (2, 4), (3, 3), (3, 4),
)


def mixer_kernel(*refs):
    (tok, state, sinner, sgroup, wgate_hbm, winner_hbm, wgroup_hbm, wst, tinner, tgroup,
     biases, step_bias, decay_rate, skip_gain, norm_gain, wout, parents, path, plen, tsize,
     mixed, next_state,
     tx, ty, wsg, st, sr, states, wx, wy,
     reach, lags, vinner, vgroup, gate, values, channels, sizes, cum_t, cum, leaf_w, leaf_e,
     outs_f, sq_s, sq_r, inv, inv_x, inv_y, norm,
     nx, ny, own, sent, got, zsend_p, zsend_m, zgot_p, zgot_m, fin, land,
     loads, turn_s, turn_r, zs, zr, cs, cr, ws_s, ws_r, ss, sr_sem, near_s, near_r, far_s, far_r, own_sem, us, ur,
     bc_s, bc_r, sq_ss, sq_rs, is_, ir, ns, nr, ks, kr, vs, vr, fs, fr, store) = refs[:93]
    bufs = refs[93:]
    p = Place()
    r, h, y, x, z, c = p.r, p.h, p.y, p.x, p.z, p.c
    hy, hx = h // 4, h % 4
    turns = (
        (tx, (z // 2 * 4 + x, 2 * ((z + 2 * y) % 8) + c),
         ((z // 2 - y) % 4 * 4 + x, 2 * (2 * y + z % 2) + c)),
        (ty, (y * 4 + 2 * (z % 2) + c, 2 * ((z + x // 2) % 8) + x % 2),
         (y * 4 + 2 * ((z - x // 2) % 2) + c, 2 * ((z - (z - x // 2) % 2) % 8) + x % 2)),
    )
    moved = [jnp.logical_or(to[0] != r, to[1] != h) for _, to, _ in turns]
    goal = ((hy * 4 + x, y * 4 + hx), (y * 4 + hx, hy * 4 + x))
    away = (hy != y, hx != x)

    fetch = pltpu.make_async_copy(state, states, loads)
    fetch.start()

    sources = {"group": wgroup_hbm, "inner": winner_hbm, "gate": wgate_hbm}
    results = {"group": vgroup, "inner": vinner, "gate": gate}
    gathers, units = [], []
    for i, (name, xcol, ycol, width) in enumerate(UNITS):
        pair = []
        for j, (axis, col) in enumerate((("x", xcol), ("y", ycol))):
            n = 2 * i + j
            gathers.append(Gather(
                p, axis, sources[name].at[:, col : col + width], bufs[8 * n], 512,
                (near_s.at[n], near_r.at[n], far_s.at[n], far_r.at[n], own_sem.at[n]),
            ))
            pair.append(Unit(p, "y" if axis == "x" else "x", gathers[-1], col, width, (tx, ty)[j],
                             results[name], bufs[8 * n + 1 : 8 * n + 8], us.at[n], ur.at[n]))
        units.append(pair)
    for j, (axis, full) in enumerate((("x", wx), ("y", wy))):
        n = 2 * len(UNITS) + j
        gathers.append(Gather(
            p, axis, wout.at[:, 256 * j : 256 * j + 256], full, 1024,
            (near_s.at[n], near_r.at[n], far_s.at[n], far_r.at[n], own_sem.at[n]),
        ))

    def start(i):
        for one in gathers[2 * i : 2 * i + 2]:
            one.start()

    def forward(i):
        for one in gathers[2 * i : 2 * i + 2]:
            one.forward()

    meet(
        [p.at(dy=d) for d in (1, 2, 3)] + [p.at(dx=d) for d in (1, 2, 3)]
        + [p.at(dz=1), p.at(dz=-1), p.at(dc=1)],
        [(turns[0][2], moved[0]), (turns[1][2], moved[1]), (goal[0], away[0]), (goal[1], away[1])],
    )

    def place_x(dz):
        zz = (z + dz) % 8
        return (zz // 2 - y) % 4, 2 * (zz % 2) + c

    def place_y(dz):
        zz = (z + dz) % 8
        high = (zz - x // 2) % 2
        return 2 * high + c, (zz - high) % 8 // 2

    def slot(j, dz):
        return tx.at[place_x(dz)] if j == 0 else ty.at[place_y(dz)]

    def turn_send(j):
        full, to, _ = turns[j]
        there = (y, 2 * (z % 2) + c) if j == 0 else (x, z // 2)
        return remote(tok, full.at[there], turn_s.at[j], turn_r.at[j], to)

    for j in range(2):

        @pl.when(moved[j])
        def _():
            turn_send(j).start()

        @pl.when(jnp.logical_not(moved[j]))
        def _():
            pltpu.make_async_copy(tok, slot(j, 0), turn_s.at[j]).start()

    start(0)
    start(1)
    start(2)
    small = []
    for d in (1, 2, 3):
        copy = remote(wst, wsg.at[x], ws_s.at[d - 1], ws_r.at[d - 1], p.at(dx=d))
        copy.start()
        small.append(copy)
    wsg[x] = wst[...]

    tree_setup(parents, reach, lags, ((sinner, vinner), (sgroup, vgroup)))

    for j in range(2):

        @pl.when(moved[j])
        def _():
            turn_send(j).wait()

        @pl.when(jnp.logical_not(moved[j]))
        def _():
            pltpu.make_async_copy(tok, slot(j, 0), turn_s.at[j]).wait()

    cores, ring = [], {}

    def to_core(j, dz):
        k = len(cores)
        copy = remote(slot(j, dz), slot(j, dz), cs.at[k], cr.at[k], p.at(dc=1))
        copy.start()
        cores.append(copy)

    def hop(d, s, j, i):
        k = len(ring)
        ref = slot(j, -s * d).at[64 * i : 64 * i + 64]
        ring[d, s, j, i] = remote(ref, ref, zs.at[k], zr.at[k], p.at(dz=d))
        ring[d, s, j, i].start()

    for s in range(4):
        for j in range(2):
            for i in range(2):
                for d in (1, -1):
                    if s > 0:
                        ring[d, s - 1, j, i].wait_recv()
                    if s < 3 or (d == 1) == (i == 0):
                        hop(d, s, j, i)
            to_core(j, -s)
            if s > 0:
                to_core(j, s)
        if s == 0:
            forward(0)
            start(3)
        if s == 1:
            forward(1)
            forward(2)
            start(4)
        if s == 2:
            forward(3)
        if s == 3:
            forward(4)
    for j in range(2):
        ring[1, 3, j, 0].wait_recv()
        ring[-1, 3, j, 1].wait_recv()
        to_core(j, 4)
    for copy in cores:
        copy.wait_recv()

    swap = remote(values.at[c], values.at[c], bc_s, bc_r, p.at(dc=1))
    tail = sr.at[1:4]
    spread = []

    def part_of_norm(k):
        at = slice(256 * k, 256 * k + 256)
        gated = outs_f[:, at] * silu(gate[:, at].astype(F32))
        norm[k] = (gated * norm_gain[0:1, at]).astype(BF16)
        for d in (1, 3, 2):
            for full, peer in ((ny.at[y, k], p.at(dy=d)), (nx.at[x, k], p.at(dx=d))):
                n = len(spread)
                copy = remote(norm.at[k], full, ns.at[n], nr.at[n], peer)
                copy.start()
                spread.append(copy)
        nx[x, k] = norm[k]
        ny[y, k] = norm[k]
        return gated[:, 0:128] * gated[:, 0:128] + gated[:, 128:256] * gated[:, 128:256]

    squares = jnp.zeros((128, 128), F32)
    for stage, unit in ORDER:
        for one in units[unit]:
            getattr(one, "stage%d" % stage)()
        if (stage, unit) == (1, 2):
            for copy in small:
                copy.wait_recv()
            raw = None
            for k in range(4):
                rows = jnp.concatenate([tx[b, k] for b in range(4)], axis=0)
                term = dot_nt(rows, wsg[k])
                raw = term if raw is None else raw + term
            for b in range(4):
                st[b] = raw[128 * b : 128 * b + 128].T
            for d in (1, 2, 3):
                remote(st.at[(y + d) % 4], sr.at[d], ss, sr_sem, p.at(dy=d)).start()

        if stage == 3 and unit in (3, 4):
            for one in units[unit]:
                squares = squares + part_of_norm(one.column // 256)
        if (stage, unit) == (3, 0):
            values[c] = tree_conv(vgroup, lags, tgroup, biases[0:1, 1024:1280], 0, 256)
            swap.start()
            pltpu.make_async_copy(tail, tail, sr_sem).wait()
            sums = st[y]
            for j in range(1, 4):
                sums = sums + sr[j]
            tree_steps(sums, step_bias, decay_rate, reach, path, plen, sizes, cum_t, cum, leaf_w, leaf_e)
        if stage == 3 and unit in (1, 2):
            for one in units[unit]:
                lo = one.column
                channels[:, lo : lo + 256] = tree_conv(
                    vinner, lags, tinner, biases[0:1, lo : lo + 256], lo, 256
                )
        if (stage, unit) == (2, 4):
            start(5)
            swap.wait_recv()
            fetch.wait()
            tree_outputs(values, states, channels, sizes, cum_t, cum, reach, skip_gain, tsize, outs_f)
            forward(5)

    sq_s[...] = jnp.broadcast_to(jnp.sum(squares.T, axis=0, keepdims=True), (8, 128))
    trade = remote(sq_s, sq_r, sq_ss, sq_rs, p.at(dc=1))
    trade.start()
    trade.wait_recv()
    inv[...] = lax.rsqrt((sq_s[...] + sq_r[...]) / GROUP_WIDTH + 1e-05)
    rates = []
    for d in (1, 3, 2):
        for full, peer in ((inv_y.at[y], p.at(dy=d)), (inv_x.at[x], p.at(dx=d))):
            n = len(rates)
            copy = remote(inv, full, is_.at[n], ir.at[n], peer)
            copy.start()
            rates.append(copy)
    inv_x[x] = inv[...]
    inv_y[y] = inv[...]
    for one in gathers[10:12]:
        one.ready()
    for copy in spread + rates:
        copy.wait_recv()

    def shard(dz, cc, half):
        s = 2 * ((z + dz) % 8) + cc
        i, j = s // 4, s % 4
        rows, scale, weight = ((ny, inv_y, wx), (nx, inv_x, wy))[half]
        a, b = (i, j) if half == 0 else (j, i)
        total = dot(rows[a, 0], weight[b, 0:256])
        for k in range(1, 4):
            total = total + dot(rows[a, k], weight[b, 256 * k : 256 * k + 256])
        return total * scale[a].T[:, 0:1]

    passed = {}

    def give(dz):
        k = dz % 8
        for half in (0, 1):
            sent[k, half] = shard(dz, 1 - c, half).astype(BF16)
        passed[k] = remote(sent.at[k], got.at[k], ks.at[k], kr.at[k], p.at(dc=1))
        passed[k].start()

    def keep(dz):
        k = dz % 8
        for half in (0, 1):
            own[k, half] = shard(dz, c, half)

    def add(dz):
        k = dz % 8
        passed[k].wait_recv()
        for half in (0, 1):
            own[k, half] = own[k, half] + got[k, half].astype(F32)

    moves = []

    def move(src, dst, d):
        k = len(moves)
        copy = remote(src, dst, vs.at[k], vr.at[k], p.at(dz=d))
        copy.start()
        moves.append(copy)
        return copy

    stores = []

    def grow(k):
        q, part = k // 2, k % 2
        advance(q, part, states, channels, values, leaf_w, leaf_e)
        ref = slice(512 * part, 512 * part + 512)
        copy = pltpu.make_async_copy(states.at[q, ref], next_state.at[q, ref], store.at[k])
        copy.start()
        stores.append(copy)

    sends, gots = {1: zsend_p, -1: zsend_m}, {1: zgot_p, -1: zgot_m}
    chain = {}

    def step(d, s, half, fresh):
        k = (d * (4 - s)) % 8
        total = own[k, half]
        if not fresh:
            chain[d, half].wait_recv()
            total = total + gots[d][s - 1, half].astype(F32)
        sends[d][s, half] = total.astype(BF16)
        chain[d, half] = move(sends[d].at[s, half], gots[d].at[s, half], d)

    give(4)
    give(3)
    give(-3)
    keep(4)
    keep(3)
    keep(-3)
    add(4)
    step(1, 0, 0, True)
    step(-1, 0, 1, True)
    add(3)
    step(1, 1, 1, True)
    add(-3)
    step(-1, 1, 0, True)
    give(2)
    give(-2)
    keep(2)
    keep(-2)
    step(1, 1, 0, False)
    step(-1, 1, 1, False)
    add(2)
    add(-2)
    step(1, 2, 1, False)
    step(-1, 2, 0, False)
    give(1)
    give(-1)
    give(0)
    keep(1)
    keep(-1)
    step(1, 2, 0, False)
    step(-1, 2, 1, False)
    add(1)
    add(-1)
    step(1, 3, 1, False)
    step(-1, 3, 0, False)
    keep(0)
    grow(0)
    step(1, 3, 0, False)
    step(-1, 3, 1, False)
    add(0)
    grow(1)

    def home(half):
        return remote(fin.at[half], land.at[half], fs.at[half], fr.at[half], goal[half])

    for half in (0, 1):
        chain[1, half].wait_recv()
        chain[-1, half].wait_recv()
        fin[half] = (
            own[0, half] + zgot_p[3, half].astype(F32) + zgot_m[3, half].astype(F32)
        ).astype(BF16)

        @pl.when(away[half])
        def _():
            home(half).start()

        @pl.when(jnp.logical_not(away[half]))
        def _():
            land[half] = fin[half]

    grow(2)
    grow(3)
    for pair in units:
        for one in pair:
            one.finish()
    pltpu.make_async_copy(tail, tail, ss).wait()
    for one in gathers:
        one.finish()
    for copy in cores + list(ring.values()) + small + [swap, trade]:
        copy.wait_send()
    for copy in spread + rates + list(passed.values()) + moves:
        copy.wait_send()
    for copy in stores:
        copy.wait()
    for half in (0, 1):

        @pl.when(away[half])
        def _():
            home(half).wait()

        mixed[:, 256 * half : 256 * half + 256] = land[half]


def mixer(*args):
    vmem = pl.BlockSpec(memory_space=pltpu.VMEM)
    smem = pl.BlockSpec(memory_space=pltpu.SMEM)
    hbm = pl.BlockSpec(memory_space=pl.ANY)
    dma = pltpu.SemaphoreType.DMA

    def flat(*shape):
        return pltpu.VMEM(shape, F32)

    def half(*shape):
        return pltpu.VMEM(shape, BF16)

    scratch = [
        half(4, 4, 128, 512), half(4, 4, 128, 512), half(4, 16, 512), flat(4, 16, 128),
        flat(4, 16, 128), flat(2, 1024, 256),
        half(4, 1024, 256), half(4, 1024, 256),
        flat(128, 128), half(384, 256), half(256, 1024), half(256, 256), half(128, 1024),
        flat(2, 128, 256), flat(128, 1024), flat(16, 128), flat(16, 128), flat(128, 16),
        flat(128, 16), flat(16, 256), flat(128, 1024), flat(8, 128), flat(8, 128),
        flat(8, 128), flat(4, 8, 128), flat(4, 8, 128), half(4, 128, 256),
        half(4, 4, 128, 256), half(4, 4, 128, 256), flat(8, 2, 128, 256),
        half(8, 2, 128, 256), half(8, 2, 128, 256),
        half(4, 2, 128, 256), half(4, 2, 128, 256), half(4, 2, 128, 256), half(4, 2, 128, 256),
        half(2, 128, 256), half(2, 128, 256),
        dma, dma((2,)), dma((2,)), dma((28,)), dma((28,)), dma((16,)), dma((16,)), dma((3,)), dma((3,)), dma, dma,
        dma((12, 4)), dma((12, 4)), dma((12, 2)), dma((12, 2)), dma((12,)),
        dma((2 * len(UNITS), 4)), dma((2 * len(UNITS), 4)),
        dma, dma, dma, dma, dma((6,)), dma((6,)), dma((24,)), dma((24,)), dma((8,)), dma((8,)),
        dma((14,)), dma((14,)), dma((2,)), dma((2,)), dma((4,)),
    ]
    for _, _, _, width in UNITS:
        scratch += ([half(4, 512, width)] + unit_scratch(width)) * 2
    shape = jax.ShapeDtypeStruct
    return pl.pallas_call(
        mixer_kernel,
        name="mixer",
        out_shape=(shape((128, 512), BF16), shape((2, 1024, 256), F32)),
        in_specs=[vmem, hbm, vmem, vmem, hbm, hbm, hbm] + [vmem] * 8 + [hbm, vmem, vmem, smem, smem],
        out_specs=(vmem, hbm),
        scratch_shapes=scratch,
        compiler_params=pltpu.CompilerParams(
            collective_id=0, has_side_effects=True, vmem_limit_bytes=58 * 2**20
        ),
    )(*args)


def on_device(
    tokens, prior_state, conv_inner_state, conv_group_state, gate_weight, inner_weight,
    group_weight, step_weight, conv_inner_weight, conv_inner_bias, conv_group_weight,
    conv_group_bias, step_bias, decay_rate, skip_gain, norm_gain, out_weight, parents,
    accepted_path, path_length, tree_size,
):
    def row(vector):
        return vector.reshape(1, -1)

    mixed, state = mixer(
        tokens, prior_state.reshape(2, 1024, 256), conv_inner_state.swapaxes(0, 1),
        conv_group_state.swapaxes(0, 1), gate_weight, inner_weight, group_weight, step_weight.T,
        conv_inner_weight, conv_group_weight,
        row(lax.optimization_barrier(
            jnp.concatenate((conv_inner_bias.astype(F32), conv_group_bias.astype(F32)))
        )),
        row(step_bias), row(decay_rate), row(skip_gain), row(norm_gain), out_weight, parents,
        accepted_path, path_length, tree_size,
    )
    return mixed, state.reshape(prior_state.shape)


def solution(mesh):
    in_specs = (
        P("req", "head"),
        P("req", "head", None, None),
        P("req", None, "head"),
        P("req", None, "head"),
        P("req", "head"),
        P("req", "head"),
        P("req", "head"),
        P("req", "head"),
        P(None, "head"),
        P("head"),
        P(None, "head"),
        P("head"),
        P("head"),
        P("head"),
        P("head"),
        P("head"),
        P("head", "req"),
        P("req", None),
        P("req", None),
        P("req"),
        P("req"),
    )
    out_specs = (P("req", "head"), P("req", "head", None, None))
    return jax.shard_map(
        on_device, mesh=mesh, in_specs=in_specs, out_specs=out_specs, check_vma=False
    )
```

```python
import functools

import jax
import jax.numpy as jnp
from jax import lax
from jax.experimental import pallas as pl
from jax.experimental.pallas import tpu as pltpu
from jax.sharding import PartitionSpec as P

GROUP_WIDTH = 2048
MESH = pl.DeviceIdType.MESH
F32 = jnp.float32
BF16 = jnp.bfloat16
HIGHEST = lax.Precision.HIGHEST
TREE_PRECISION = HIGHEST
UNITS = (
    ("group", 0, 128, 128),
    ("inner", 0, 512, 256),
    ("inner", 256, 768, 256),
    ("gate", 0, 512, 256),
    ("gate", 256, 768, 256),
)


class Place:
    def __init__(self):
        self.r = lax.axis_index("req")
        self.h = lax.axis_index("head")
        self.y, self.x = self.r // 4, self.r % 4
        self.z, self.c = self.h // 2, self.h % 2

    def at(self, dy=0, dx=0, dz=0, dc=0):
        y, x = (self.y + dy) % 4, (self.x + dx) % 4
        z, c = (self.z + dz) % 8, (self.c + dc) % 2
        return (y * 4 + x, z * 2 + c)


def remote(src, dst, send, recv, device):
    return pltpu.make_async_remote_copy(
        src_ref=src, dst_ref=dst, send_sem=send, recv_sem=recv,
        device_id=device, device_id_type=MESH,
    )


def meet(devices, maybe=()):
    barrier = pltpu.get_barrier_semaphore()
    for device in devices:
        pl.semaphore_signal(barrier, inc=1, device_id=device, device_id_type=MESH)
    for device, here in maybe:
        @pl.when(here)
        def _():
            pl.semaphore_signal(barrier, inc=1, device_id=device, device_id_type=MESH)
    pl.semaphore_wait(barrier, len(devices) + sum(jnp.where(here, 1, 0) for _, here in maybe))


def dot(a, b, precision=None):
    return jnp.dot(a, b, preferred_element_type=F32, precision=precision)


def dot_nt(a, b, precision=None):
    return lax.dot_general(
        a, b, (((1,), (1,)), ((), ())), preferred_element_type=F32, precision=precision
    )


def dot_tn(a, b, precision=None):
    return lax.dot_general(
        a, b, (((0,), (0,)), ((), ())), preferred_element_type=F32, precision=precision
    )


def silu(u):
    return u / (1.0 + jnp.exp(-u))


def iota(shape, axis):
    return lax.broadcasted_iota(jnp.int32, shape, axis)


class Gather:
    def __init__(self, place, axis, block, full, rows, sems):
        self.p, self.axis, self.block, self.full, self.rows = place, axis, block, full, rows
        self.me = place.x if axis == "x" else place.y
        self.near_s, self.near_r, self.far_s, self.far_r, self.own = sems
        self.near, self.far = [], []

    def peer(self, d):
        return self.p.at(dx=d) if self.axis == "x" else self.p.at(dy=d)

    def halves(self, d):
        half = self.rows // 2
        first = 0 if d == 1 else half
        return pl.ds(first, half), pl.ds(half - first, half)

    def load(self):
        self.keep = pltpu.make_async_copy(self.block, self.full.at[self.me], self.own)
        self.keep.start()

    def start(self):
        self.keep.wait()
        for n in range(2):
            for i, d in enumerate((1, -1)):
                rows, k = self.halves(d)[n], 2 * n + i
                self.near.append(remote(
                    self.full.at[self.me, rows], self.full.at[self.me, rows],
                    self.near_s.at[k], self.near_r.at[k], self.peer(d),
                ))
                self.near[-1].start()

    def forward(self):
        for i, d in enumerate((1, -1)):
            self.near[i].wait_recv()
            ref = self.full.at[(self.me - d) % 4, self.halves(d)[0]]
            self.far.append(remote(ref, ref, self.far_s.at[i], self.far_r.at[i], self.peer(d)))
            self.far[-1].start()

    def ready(self):
        for copy in self.near[2:] + self.far:
            copy.wait_recv()

    def finish(self):
        for copy in self.near + self.far:
            copy.wait_send()


class Unit:
    def __init__(self, place, along, gather, column, width, tokens, out, bufs, send, recv):
        self.p, self.along = place, along
        self.b = place.y if along == "y" else place.x
        self.gather, self.column, self.width = gather, column, width
        self.tokens, self.out = tokens, out
        self.q, self.s3, self.rh, self.s4p, self.s4m, self.rip, self.rim = bufs
        self.send, self.recv = send, recv
        self.copies = {}

    def put(self, k, src, dst, step):
        peer = self.p.at(dy=step) if self.along == "y" else self.p.at(dx=step)
        copy = remote(src, dst, self.send.at[k], self.recv.at[k], peer)
        copy.start()
        self.copies[k] = copy

    def stage1(self):
        self.gather.ready()
        total = None
        for k in range(4):
            rows = jnp.concatenate([self.tokens[b, k] for b in range(4)], axis=0)
            term = dot(rows, self.gather.full[k])
            total = term if total is None else total + term
        for b in range(4):
            self.q[b] = total[128 * b : 128 * b + 128]
        self.s3[...] = self.q[(self.b + 2) % 4].astype(BF16)
        self.put(0, self.s3.at[0:64], self.rh.at[0:64], 1)
        self.put(1, self.s3.at[64:128], self.rh.at[64:128], -1)

    def stage2(self):
        self.copies[0].wait_recv()
        self.copies[1].wait_recv()
        up, down = (self.b + 1) % 4, (self.b + 3) % 4
        self.s4p[0:64] = (self.q[up, 0:64] + self.rh[0:64].astype(F32)).astype(BF16)
        self.s4p[64:128] = self.q[up, 64:128].astype(BF16)
        self.s4m[0:64] = self.q[down, 0:64].astype(BF16)
        self.s4m[64:128] = (self.q[down, 64:128] + self.rh[64:128].astype(F32)).astype(BF16)
        self.put(2, self.s4p, self.rip, 1)
        self.put(3, self.s4m, self.rim, -1)

    def stage3(self):
        self.copies[2].wait_recv()
        self.copies[3].wait_recv()
        total = self.q[self.b] + self.rip[...].astype(F32) + self.rim[...].astype(F32)
        self.out[0:128, self.column : self.column + self.width] = total.astype(BF16)

    def finish(self):
        for copy in self.copies.values():
            copy.wait_send()


def unit_scratch(width):
    flat = pltpu.VMEM((128, width), BF16)
    return [pltpu.VMEM((4, 128, width), F32)] + [flat] * 6


def tree_setup(parents, reach, lags, priors):
    lane = iota((1, 128), 1)
    own = jnp.concatenate((parents[0:1], parents[1:2]), axis=1)
    own = jnp.where(own < 0, -1, jnp.where(lane < 64, own, own + 64))
    parent = (iota((128, 128), 0) == own).astype(F32).T
    step = parent.astype(BF16)
    covered = (iota((128, 128), 0) == iota((128, 128), 1)).astype(F32) + parent
    for _ in range(6):
        half = covered.astype(BF16)
        covered = jnp.minimum(dot(half, half), 1.0)
    reach[...] = covered
    depth = jnp.sum(covered, axis=1, keepdims=True).astype(jnp.int32) - 1
    row, col = iota((128, 128), 0), iota((128, 128), 1)
    same = (col < 6) & (row // 64 == col // 3)
    ancestor = step
    for k in range(1, 4):
        if k > 1:
            ancestor = dot(ancestor, step).astype(BF16)
        prior = same & (k > depth) & (col % 3 == 3 - k + depth)
        lags[128 * (k - 1) : 128 * k, 0:128] = ancestor
        lags[128 * (k - 1) : 128 * k, 128:256] = prior.astype(F32).astype(BF16)
    for prior, values in priors:
        width = values.shape[1]
        both = [prior[k].astype(F32) for k in range(3)]
        six = [both[k][q : q + 1] for q in range(2) for k in range(3)]
        six = jnp.concatenate(six + [jnp.zeros((2, width), F32)], axis=0)
        values[128:256] = jnp.concatenate((six, jnp.zeros((120, width), F32)), axis=0).astype(BF16)


def tree_conv(values, lags, taps, bias, lo, width):
    at = slice(lo, lo + width)
    earlier = dot(lags[...], values[:, at])
    taps = taps[:, at].astype(F32)
    total = bias + taps[3:4] * values[0:128, at].astype(F32)
    for k in range(1, 4):
        total = total + taps[3 - k : 4 - k] * earlier[128 * (k - 1) : 128 * k]
    return silu(total)


def as_column(row):
    n = row.shape[1]
    return jnp.sum(jnp.where(iota((n, n), 0) == iota((n, n), 1), row, 0.0), axis=1, keepdims=True)


def tree_steps(sums, bias, rate, reach, path, plen, sizes, cum_t, cum, leaf_w, leaf_e):
    raw = sums.astype(BF16).astype(F32) + as_column(bias[...])
    size = jnp.maximum(raw, 0.0) + jnp.log1p(jnp.exp(-jnp.abs(raw)))
    log_decay = -as_column(rate[...]) * size
    total = dot_nt(log_decay, reach[...], HIGHEST)
    sizes[...] = size
    cum_t[...] = total
    cum[...] = total.T
    weights = jnp.zeros((16, 128), F32)
    for q in range(2):
        last = iota((1, 64), 1) == plen[q] - 1
        leaf = jnp.sum(jnp.where(last, path[q : q + 1], 0), axis=1, keepdims=True) + 64 * q
        here = (iota((1, 128), 1) == leaf).astype(F32)
        above = dot(here.astype(BF16), reach[...].astype(BF16))
        at_leaf = jnp.sum(here * total, axis=1, keepdims=True)
        weights = weights + jnp.where(above > 0, jnp.exp(jnp.minimum(at_leaf - total, 0.0)), 0.0)
        leaf_e[:, 128 * q : 128 * q + 128] = jnp.broadcast_to(jnp.exp(at_leaf), (16, 128))
    leaf_w[...] = (weights * size).T


def tree_mixes(values, states, sizes, cum_t, cum, reach, mixes, out):
    c_half = values[1].astype(BF16)
    meet_bc = dot_nt(c_half, values[0].astype(BF16))
    linked = reach[...] > 0
    for head in range(16):
        column, across = cum[:, head : head + 1], cum_t[head : head + 1]
        decay = jnp.where(linked, jnp.exp(jnp.minimum(column - across, 0.0)), 0.0)
        mixes[head // 2, :, 128 * (head % 2) : 128 * (head % 2) + 128] = (
            decay * meet_bc * sizes[head : head + 1]
        ).astype(BF16)
    for q in range(2):
        rows = slice(64 * q, 64 * q + 64)
        out[rows] = dot_nt(c_half[rows], states[q].astype(BF16))


def tree_outputs(pairs, channels, cum, mixes, gain, tsize, out):
    lane = iota((128, 128), 1) < 64
    row = iota((128, 1), 0)
    valid = jnp.where(row < 64, row, row - 64) < jnp.where(row < 64, tsize[0], tsize[1])
    for pair in pairs:
        at = slice(128 * pair, 128 * pair + 128)
        x = channels[:, at]
        heads = (2 * pair, 2 * pair + 1)
        grown = [jnp.exp(cum[:, head : head + 1]) for head in heads]
        skips = [gain[0:1, head : head + 1] for head in heads]
        both = dot(
            mixes[pair],
            jnp.concatenate(
                (jnp.where(lane, x, 0.0).astype(BF16), jnp.where(lane, 0.0, x).astype(BF16)), axis=0
            ),
        )
        total = both + jnp.where(lane, grown[0], grown[1]) * out[:, at]
        total = total + jnp.where(lane, skips[0], skips[1]) * x
        out[:, at] = jnp.where(valid, total, 0.0)


def advance(q, part, states, channels, values, leaf_w, leaf_e):
    rows = slice(64 * q, 64 * q + 64)
    lane = iota((64, 128), 1) < 64
    for pair in range(4 * part, 4 * part + 4):
        at = slice(128 * pair, 128 * pair + 128)
        weight = jnp.where(
            lane, leaf_w[rows, 2 * pair : 2 * pair + 1], leaf_w[rows, 2 * pair + 1 : 2 * pair + 2]
        )
        added = dot_tn(channels[rows, at] * weight, values[0, rows], TREE_PRECISION)
        for j in range(2):
            head = 2 * pair + j
            kept = leaf_e[head : head + 1, 128 * q : 128 * q + 1]
            block = slice(64 * head, 64 * head + 64)
            states[q, block] = kept * states[q, block] + added[64 * j : 64 * j + 64]


ORDER = (
    (1, 0), (1, 1), (2, 0), (1, 2), (3, 0), (2, 1), (1, 3), (2, 2), (1, 4), (2, 3), (3, 1), (2, 4),
    (3, 2), (3, 3), (3, 4),
)


def mixer_kernel(*refs):
    (tok, state, sinner, sgroup, wgate_hbm, winner_hbm, wgroup_hbm, wst, tinner, tgroup,
     biases, step_bias, decay_rate, skip_gain, norm_gain, wout, parents, path, plen, tsize,
     mixed, next_state,
     tx, ty, wsg, st, sr, states, wx, wy,
     reach, lags, vinner, vgroup, gate, values, channels, sizes, cum_t, cum, leaf_w, leaf_e, mixes,
     outs_f, sq_s, sq_r, inv, inv_x, inv_y, norm,
     nx, ny, own, sent, got, zsend_p, zsend_m, zgot_p, zgot_m, fin, land,
     loads, turn_s, turn_r, zs, zr, cs, cr, ws_s, ws_r, ss, sr_sem, near_s, near_r, far_s, far_r, own_sem, us, ur,
     bc_s, bc_r, sq_ss, sq_rs, is_, ir, ns, nr, ks, kr, vs, vr, fs, fr, store) = refs[:94]
    bufs = refs[94:]
    p = Place()
    r, h, y, x, z, c = p.r, p.h, p.y, p.x, p.z, p.c
    hy, hx = h // 4, h % 4
    turns = (
        (tx, (z // 2 * 4 + x, 2 * ((z + 2 * y) % 8) + c),
         ((z // 2 - y) % 4 * 4 + x, 2 * (2 * y + z % 2) + c)),
        (ty, (y * 4 + 2 * (z % 2) + c, 2 * ((z + x // 2) % 8) + x % 2),
         (y * 4 + 2 * ((z - x // 2) % 2) + c, 2 * ((z - (z - x // 2) % 2) % 8) + x % 2)),
    )
    moved = [jnp.logical_or(to[0] != r, to[1] != h) for _, to, _ in turns]
    goal = ((hy * 4 + x, y * 4 + hx), (y * 4 + hx, hy * 4 + x))
    away = (hy != y, hx != x)

    fetch = pltpu.make_async_copy(state, states, loads)

    sources = {"group": wgroup_hbm, "inner": winner_hbm, "gate": wgate_hbm}
    results = {"group": vgroup, "inner": vinner, "gate": gate}
    gathers, units = [], []
    for i, (name, xcol, ycol, width) in enumerate(UNITS):
        pair = []
        for j, (axis, col) in enumerate((("x", xcol), ("y", ycol))):
            n = 2 * i + j
            gathers.append(Gather(
                p, axis, sources[name].at[:, col : col + width], bufs[8 * n], 512,
                (near_s.at[n], near_r.at[n], far_s.at[n], far_r.at[n], own_sem.at[n]),
            ))
            pair.append(Unit(p, "y" if axis == "x" else "x", gathers[-1], col, width, (tx, ty)[j],
                             results[name], bufs[8 * n + 1 : 8 * n + 8], us.at[n], ur.at[n]))
        units.append(pair)
    for j, (axis, full) in enumerate((("x", wx), ("y", wy))):
        n = 2 * len(UNITS) + j
        gathers.append(Gather(
            p, axis, wout.at[:, 256 * j : 256 * j + 256], full, 1024,
            (near_s.at[n], near_r.at[n], far_s.at[n], far_r.at[n], own_sem.at[n]),
        ))

    def start(i):
        for one in gathers[2 * i : 2 * i + 2]:
            one.start()

    def forward(i):
        for one in gathers[2 * i : 2 * i + 2]:
            one.forward()

    for one in gathers:
        one.load()
    fetch.start()
    meet(
        [p.at(dy=d) for d in (1, 2, 3)] + [p.at(dx=d) for d in (1, 2, 3)]
        + [p.at(dz=1), p.at(dz=-1), p.at(dc=1)],
        [(turns[0][2], moved[0]), (turns[1][2], moved[1]), (goal[0], away[0]), (goal[1], away[1])],
    )

    def place_x(dz):
        zz = (z + dz) % 8
        return (zz // 2 - y) % 4, 2 * (zz % 2) + c

    def place_y(dz):
        zz = (z + dz) % 8
        high = (zz - x // 2) % 2
        return 2 * high + c, (zz - high) % 8 // 2

    def slot(j, dz):
        return tx.at[place_x(dz)] if j == 0 else ty.at[place_y(dz)]

    def turn_send(j):
        full, to, _ = turns[j]
        there = (y, 2 * (z % 2) + c) if j == 0 else (x, z // 2)
        return remote(tok, full.at[there], turn_s.at[j], turn_r.at[j], to)

    for j in range(2):

        @pl.when(moved[j])
        def _():
            turn_send(j).start()

        @pl.when(jnp.logical_not(moved[j]))
        def _():
            pltpu.make_async_copy(tok, slot(j, 0), turn_s.at[j]).start()

    start(0)
    start(1)
    start(2)
    start(3)
    start(4)
    small = []
    for d in (1, 2, 3):
        copy = remote(wst, wsg.at[x], ws_s.at[d - 1], ws_r.at[d - 1], p.at(dx=d))
        copy.start()
        small.append(copy)
    wsg[x] = wst[...]

    tree_setup(parents, reach, lags, ((sinner, vinner), (sgroup, vgroup)))

    cores, ring = [], {}

    def to_core(j, dz):
        k = len(cores)
        copy = remote(slot(j, dz), slot(j, dz), cs.at[k], cr.at[k], p.at(dc=1))
        copy.start()
        cores.append(copy)

    def hop(d, s, j, i):
        k = len(ring)
        ref = slot(j, -s * d).at[64 * i : 64 * i + 64]
        ring[d, s, j, i] = remote(ref, ref, zs.at[k], zr.at[k], p.at(dz=d))
        ring[d, s, j, i].start()

    for s in range(4):
        for j in (1, 0):
            if s == 0:

                @pl.when(moved[j])
                def _():
                    turn_send(j).wait()

                @pl.when(jnp.logical_not(moved[j]))
                def _():
                    pltpu.make_async_copy(tok, slot(j, 0), turn_s.at[j]).wait()

            for i in range(2):
                for d in (1, -1):
                    if s > 0:
                        ring[d, s - 1, j, i].wait_recv()
                    if s < 3 or (d == 1) == (i == 0):
                        hop(d, s, j, i)
            to_core(j, -s)
            if s > 0:
                to_core(j, s)
        if s == 0:
            forward(0)
        if s == 1:
            forward(1)
            forward(2)
        if s == 2:
            forward(3)
    forward(4)
    start(5)
    for j in (1, 0):
        ring[1, 3, j, 0].wait_recv()
        ring[-1, 3, j, 1].wait_recv()
        to_core(j, 4)
    for copy in cores:
        copy.wait_recv()

    swap = remote(values.at[c], values.at[c], bc_s, bc_r, p.at(dc=1))
    tail = sr.at[1:4]
    spread = []

    def part_of_norm(k):
        at = slice(256 * k, 256 * k + 256)
        gated = outs_f[:, at] * silu(gate[:, at].astype(F32))
        norm[k] = (gated * norm_gain[0:1, at]).astype(BF16)
        for d in (1, 3, 2):
            for full, peer in ((ny.at[y, k], p.at(dy=d)), (nx.at[x, k], p.at(dx=d))):
                n = len(spread)
                copy = remote(norm.at[k], full, ns.at[n], nr.at[n], peer)
                copy.start()
                spread.append(copy)
        nx[x, k] = norm[k]
        ny[y, k] = norm[k]
        return gated[:, 0:128] * gated[:, 0:128] + gated[:, 128:256] * gated[:, 128:256]

    squares = jnp.zeros((128, 128), F32)
    for stage, unit in ORDER:
        for one in units[unit]:
            getattr(one, "stage%d" % stage)()
        if (stage, unit) == (1, 1):
            for copy in small:
                copy.wait_recv()
            raw = None
            for k in range(4):
                rows = jnp.concatenate([tx[b, k] for b in range(4)], axis=0)
                term = dot_nt(rows, wsg[k])
                raw = term if raw is None else raw + term
            for b in range(4):
                st[b] = raw[128 * b : 128 * b + 128].T
            for d in (1, 2, 3):
                remote(st.at[(y + d) % 4], sr.at[d], ss, sr_sem, p.at(dy=d)).start()

        if stage == 3 and unit in (3, 4):
            for one in units[unit]:
                squares = squares + part_of_norm(one.column // 256)
        if (stage, unit) == (3, 0):
            values[c] = tree_conv(vgroup, lags, tgroup, biases[0:1, 1024:1280], 0, 256)
            swap.start()
            pltpu.make_async_copy(tail, tail, sr_sem).wait()
            sums = st[y]
            for j in range(1, 4):
                sums = sums + sr[j]
            tree_steps(sums, step_bias, decay_rate, reach, path, plen, sizes, cum_t, cum, leaf_w, leaf_e)
        if stage == 3 and unit in (1, 2):
            for one in units[unit]:
                lo = one.column
                channels[:, lo : lo + 256] = tree_conv(
                    vinner, lags, tinner, biases[0:1, lo : lo + 256], lo, 256
                )
        if (stage, unit) == (1, 4):
            swap.wait_recv()
            fetch.wait()
            tree_mixes(values, states, sizes, cum_t, cum, reach, mixes, outs_f)
        if stage == 3 and unit in (1, 2):
            for one in units[unit]:
                lo = one.column // 128
                tree_outputs((lo, lo + 1), channels, cum, mixes, skip_gain, tsize, outs_f)
        if (stage, unit) == (3, 0):
            forward(5)

    sq_s[...] = jnp.broadcast_to(jnp.sum(squares.T, axis=0, keepdims=True), (8, 128))
    trade = remote(sq_s, sq_r, sq_ss, sq_rs, p.at(dc=1))
    trade.start()
    trade.wait_recv()
    inv[...] = lax.rsqrt((sq_s[...] + sq_r[...]) / GROUP_WIDTH + 1e-05)
    rates = []
    for d in (1, 3, 2):
        for full, peer in ((inv_y.at[y], p.at(dy=d)), (inv_x.at[x], p.at(dx=d))):
            n = len(rates)
            copy = remote(inv, full, is_.at[n], ir.at[n], peer)
            copy.start()
            rates.append(copy)
    inv_x[x] = inv[...]
    inv_y[y] = inv[...]
    for one in gathers[10:12]:
        one.ready()
    for copy in spread + rates:
        copy.wait_recv()

    def shard(dz, cc, half):
        s = 2 * ((z + dz) % 8) + cc
        i, j = s // 4, s % 4
        rows, scale, weight = ((ny, inv_y, wx), (nx, inv_x, wy))[half]
        a, b = (i, j) if half == 0 else (j, i)
        total = dot(rows[a, 0], weight[b, 0:256])
        for k in range(1, 4):
            total = total + dot(rows[a, k], weight[b, 256 * k : 256 * k + 256])
        return total * scale[a].T[:, 0:1]

    passed = {}

    def give(dz):
        k = dz % 8
        for half in (0, 1):
            sent[k, half] = shard(dz, 1 - c, half).astype(BF16)
        passed[k] = remote(sent.at[k], got.at[k], ks.at[k], kr.at[k], p.at(dc=1))
        passed[k].start()

    def keep(dz):
        k = dz % 8
        for half in (0, 1):
            own[k, half] = shard(dz, c, half)

    def add(dz):
        k = dz % 8
        passed[k].wait_recv()
        for half in (0, 1):
            own[k, half] = own[k, half] + got[k, half].astype(F32)

    moves = []

    def move(src, dst, d):
        k = len(moves)
        copy = remote(src, dst, vs.at[k], vr.at[k], p.at(dz=d))
        copy.start()
        moves.append(copy)
        return copy

    stores = []

    def grow(k):
        q, part = k // 2, k % 2
        advance(q, part, states, channels, values, leaf_w, leaf_e)
        ref = slice(512 * part, 512 * part + 512)
        copy = pltpu.make_async_copy(states.at[q, ref], next_state.at[q, ref], store.at[k])
        copy.start()
        stores.append(copy)

    sends, gots = {1: zsend_p, -1: zsend_m}, {1: zgot_p, -1: zgot_m}
    chain = {}

    def step(d, s, half, fresh):
        k = (d * (4 - s)) % 8
        total = own[k, half]
        if not fresh:
            chain[d, half].wait_recv()
            total = total + gots[d][s - 1, half].astype(F32)
        sends[d][s, half] = total.astype(BF16)
        chain[d, half] = move(sends[d].at[s, half], gots[d].at[s, half], d)

    give(4)
    keep(4)
    give(3)
    add(4)
    step(1, 0, 0, True)
    step(-1, 0, 1, True)
    keep(3)
    give(-3)
    keep(-3)
    add(3)
    step(1, 1, 1, True)
    add(-3)
    step(-1, 1, 0, True)
    give(2)
    give(-2)
    keep(2)
    keep(-2)
    step(1, 1, 0, False)
    step(-1, 1, 1, False)
    add(2)
    add(-2)
    step(1, 2, 1, False)
    step(-1, 2, 0, False)
    give(1)
    give(-1)
    give(0)
    keep(1)
    keep(-1)
    step(1, 2, 0, False)
    step(-1, 2, 1, False)
    add(1)
    add(-1)
    step(1, 3, 1, False)
    step(-1, 3, 0, False)
    keep(0)
    grow(0)
    step(1, 3, 0, False)
    step(-1, 3, 1, False)
    add(0)
    grow(1)

    def home(half):
        return remote(fin.at[half], land.at[half], fs.at[half], fr.at[half], goal[half])

    for half in (0, 1):
        chain[1, half].wait_recv()
        chain[-1, half].wait_recv()
        fin[half] = (
            own[0, half] + zgot_p[3, half].astype(F32) + zgot_m[3, half].astype(F32)
        ).astype(BF16)

        @pl.when(away[half])
        def _():
            home(half).start()

        @pl.when(jnp.logical_not(away[half]))
        def _():
            land[half] = fin[half]

    grow(2)
    grow(3)
    for pair in units:
        for one in pair:
            one.finish()
    pltpu.make_async_copy(tail, tail, ss).wait()
    for one in gathers:
        one.finish()
    for copy in cores + list(ring.values()) + small + [swap, trade]:
        copy.wait_send()
    for copy in spread + rates + list(passed.values()) + moves:
        copy.wait_send()
    for copy in stores:
        copy.wait()
    for half in (0, 1):

        @pl.when(away[half])
        def _():
            home(half).wait()

        mixed[:, 256 * half : 256 * half + 256] = land[half]


def mixer(*args):
    vmem = pl.BlockSpec(memory_space=pltpu.VMEM)
    smem = pl.BlockSpec(memory_space=pltpu.SMEM)
    hbm = pl.BlockSpec(memory_space=pl.ANY)
    dma = pltpu.SemaphoreType.DMA

    def flat(*shape):
        return pltpu.VMEM(shape, F32)

    def half(*shape):
        return pltpu.VMEM(shape, BF16)

    scratch = [
        half(4, 4, 128, 512), half(4, 4, 128, 512), half(4, 16, 512), flat(4, 16, 128),
        flat(4, 16, 128), flat(2, 1024, 256),
        half(4, 1024, 256), half(4, 1024, 256),
        flat(128, 128), half(384, 256), half(256, 1024), half(256, 256), half(128, 1024),
        flat(2, 128, 256), flat(128, 1024), flat(16, 128), flat(16, 128), flat(128, 16),
        flat(128, 16), flat(16, 256), half(8, 128, 256), flat(128, 1024), flat(8, 128), flat(8, 128),
        flat(8, 128), flat(4, 8, 128), flat(4, 8, 128), half(4, 128, 256),
        half(4, 4, 128, 256), half(4, 4, 128, 256), flat(8, 2, 128, 256),
        half(8, 2, 128, 256), half(8, 2, 128, 256),
        half(4, 2, 128, 256), half(4, 2, 128, 256), half(4, 2, 128, 256), half(4, 2, 128, 256),
        half(2, 128, 256), half(2, 128, 256),
        dma, dma((2,)), dma((2,)), dma((28,)), dma((28,)), dma((16,)), dma((16,)), dma((3,)), dma((3,)), dma, dma,
        dma((12, 4)), dma((12, 4)), dma((12, 2)), dma((12, 2)), dma((12,)),
        dma((2 * len(UNITS), 4)), dma((2 * len(UNITS), 4)),
        dma, dma, dma, dma, dma((6,)), dma((6,)), dma((24,)), dma((24,)), dma((8,)), dma((8,)),
        dma((14,)), dma((14,)), dma((2,)), dma((2,)), dma((4,)),
    ]
    for _, _, _, width in UNITS:
        scratch += ([half(4, 512, width)] + unit_scratch(width)) * 2
    shape = jax.ShapeDtypeStruct
    return pl.pallas_call(
        mixer_kernel,
        name="mixer",
        out_shape=(shape((128, 512), BF16), shape((2, 1024, 256), F32)),
        in_specs=[vmem, hbm, vmem, vmem, hbm, hbm, hbm] + [vmem] * 8 + [hbm, vmem, vmem, smem, smem],
        out_specs=(vmem, hbm),
        scratch_shapes=scratch,
        compiler_params=pltpu.CompilerParams(
            collective_id=0, has_side_effects=True, vmem_limit_bytes=58 * 2**20
        ),
    )(*args)


def hand_on_kernel(mixed, state, mixed_out, state_out, mixed_here, state_here, sems, out_sems):
    pieces = [(mixed, mixed_here, mixed_out)]
    for q in range(2):
        for part in range(4):
            at = (q, pl.ds(256 * part, 256))
            pieces.append((state.at[at], state_here.at[at], state_out.at[at]))
    loads = [pltpu.make_async_copy(a, b, sems.at[k]) for k, (a, b, _) in enumerate(pieces)]
    stores = [pltpu.make_async_copy(b, c, out_sems.at[k]) for k, (_, b, c) in enumerate(pieces)]
    for copy in loads:
        copy.start()
    for load, store in zip(loads, stores):
        load.wait()
        store.start()
    for copy in stores:
        copy.wait()


def hand_on(mixed, state):
    hbm = pl.BlockSpec(memory_space=pl.ANY)
    return pl.pallas_call(
        hand_on_kernel,
        name="hand_on",
        out_shape=(
            jax.ShapeDtypeStruct(mixed.shape, mixed.dtype),
            jax.ShapeDtypeStruct(state.shape, state.dtype),
        ),
        in_specs=[hbm] * 2,
        out_specs=(hbm,) * 2,
        scratch_shapes=[
            pltpu.VMEM(mixed.shape, mixed.dtype), pltpu.VMEM(state.shape, state.dtype),
            pltpu.SemaphoreType.DMA((9,)), pltpu.SemaphoreType.DMA((9,)),
        ],
    )(mixed, state)


def on_device(
    tokens, prior_state, conv_inner_state, conv_group_state, gate_weight, inner_weight,
    group_weight, step_weight, conv_inner_weight, conv_inner_bias, conv_group_weight,
    conv_group_bias, step_bias, decay_rate, skip_gain, norm_gain, out_weight, parents,
    accepted_path, path_length, tree_size,
):
    def row(vector):
        return vector.reshape(1, -1)

    mixed, state = mixer(
        tokens, prior_state.reshape(2, 1024, 256), conv_inner_state.swapaxes(0, 1),
        conv_group_state.swapaxes(0, 1), gate_weight, inner_weight, group_weight, step_weight.T,
        conv_inner_weight, conv_group_weight,
        row(lax.optimization_barrier(
            jnp.concatenate((conv_inner_bias.astype(F32), conv_group_bias.astype(F32)))
        )),
        row(step_bias), row(decay_rate), row(skip_gain), row(norm_gain), out_weight, parents,
        accepted_path, path_length, tree_size,
    )
    mixed, state = hand_on(mixed, state)
    return mixed, state.reshape(prior_state.shape)


def solution(mesh):
    in_specs = (
        P("req", "head"),
        P("req", "head", None, None),
        P("req", None, "head"),
        P("req", None, "head"),
        P("req", "head"),
        P("req", "head"),
        P("req", "head"),
        P("req", "head"),
        P(None, "head"),
        P("head"),
        P(None, "head"),
        P("head"),
        P("head"),
        P("head"),
        P("head"),
        P("head"),
        P("head", "req"),
        P("req", None),
        P("req", None),
        P("req"),
        P("req"),
    )
    out_specs = (P("req", "head"), P("req", "head", None, None))
    return jax.shard_map(
        on_device, mesh=mesh, in_specs=in_specs, out_specs=out_specs, check_vma=False
    )
```
